32 devices in a mesh: groups: 2 (over y), particle: 4 (over z), cls: 4 (over x, core).
Axes of the slice: x: 2, y: 2, z: 4, core: 2. Of those that a mesh axis runs over, the one named last changes fastest.
Arguments:
- pool: bfloat16 [1536, 4096], P(('groups', 'particle', 'cls')), parts along dimension 0, may hold values from -48 to 48
- picks: int32 [768], P(('groups', 'particle', 'cls')), parts along dimension 0, may hold values from 0 to 47, as said below
- groups: int32 [768], P(('groups', 'particle', 'cls')), parts along dimension 0, may hold values from 0 to 63
- ctf_table: float32 [128, 32], P('groups'), parts along dimension 0, may hold values from 0.5 to 1
- shifts: int32 [72], P('groups'), parts along dimension 0, may hold values from 0 to 127, as said below
- classes: float32 [800, 4096], P(('groups', 'cls')), parts along dimension 0
- log_prior: float32 [800], P(('groups', 'cls')), parts along dimension 0, may hold values from -1 to 1
Outputs:
- new_classes: float32 [800, 4096], P(('groups', 'cls')), parts along dimension 0
- log_evidence: float32 [768], P(('groups', 'particle')), parts along dimension 0
The draws below stay inside these ranges and needn't reach their ends.
There are 2 independent parts, one for each index of `groups`. The reference program is written for one: setup_inputs(seed, part) draws one part's arguments, and reference() takes and returns one part's arrays. A program takes and returns all parts, laid end to end along the dimension named above; each array names one. Nothing has to cross between parts.
Inputs may be any that keep to these rules, and one draw needn't show every extreme that they name: `picks`: the 24 entries of each device are distinct rows of that device's own 48 pool rows, counted from its first. `shifts`: distinct angular offsets, 0 and 127 among them.
All inputs are finite; a program needn't handle non-finite values.
Results may differ from the reference program's by a relative error of at most 0.0052.
Values may be sent and summed in bfloat16 or wider, within the bound.
No kernel may reach another device: no remote copies, remote signals or barrier semaphores. Data moves between devices by JAX's collectives and lax.ppermute only.
A program may use at most 64 MiB of HBM per device.

```python
import math
import jax
import jax.numpy as jnp
from jax import lax

CYCLES = 32
ANG = 128
PIX = 4096
ROT = 36
K = 400
NGROUP = 64
BATCH_DEV = 24
POOL_DEV = 48
BATCH = 384
POOL = 768
N_CLS = 4


def class_scale():
    return max(0.05, 2.0 / math.sqrt(PIX))


def class_base(key):
    return class_scale() * jax.random.normal(jax.random.fold_in(key, 11), (K, PIX), jnp.float32)


def shift_base(key):
    inner = jax.random.permutation(jax.random.fold_in(key, 12), ANG - 2)[:ROT - 2].astype(jnp.int32) + 1
    ends = jnp.array([0, ANG - 1], dtype=jnp.int32)
    values = jnp.concatenate([ends, inner])
    order = jax.random.permutation(jax.random.fold_in(key, 19), ROT)
    return values[order].astype(jnp.int32)


def drawn_rows(key):
    power = class_scale() * class_scale() * PIX
    polar_refs = class_base(key).reshape(K, CYCLES, ANG)
    shift_table = shift_base(key)
    which = jax.random.randint(jax.random.fold_in(key, 15), (POOL,), 0, K)
    first_rot = jax.random.randint(jax.random.fold_in(key, 16), (POOL,), 0, ROT)
    second_rot = (first_rot + jax.random.randint(jax.random.fold_in(key, 17), (POOL,), 1, ROT)) % ROT
    strength = jax.random.uniform(jax.random.fold_in(key, 18), (POOL,), jnp.float32, 150.0, 400.0) / power
    picked = polar_refs[which]
    angles = jnp.arange(ANG, dtype=jnp.int32)
    first_index = (angles[None, :] - shift_table[first_rot][:, None]) % ANG
    second_index = (angles[None, :] - shift_table[second_rot][:, None]) % ANG
    first_view = jnp.take_along_axis(picked, first_index[:, None, :], axis=2)
    second_view = jnp.take_along_axis(picked, second_index[:, None, :], axis=2)
    aligned = strength[:, None, None] * first_view + (strength - 2.5 / power)[:, None, None] * second_view
    marked = (jnp.arange(POOL, dtype=jnp.int32) % 8 == 0).astype(jnp.float32)
    return marked[:, None] * aligned.reshape(POOL, PIX)


def draw_classes(key, part):
    return class_base(key)


def draw_shifts(key, part):
    return shift_base(key)


def draw_picks(key, part):
    owners = POOL // POOL_DEV
    key_list = jax.random.split(jax.random.fold_in(key, 13), owners)

    def single(owner_key):
        return jax.random.permutation(owner_key, POOL_DEV)[:BATCH_DEV]
    return jax.vmap(single)(key_list).reshape(BATCH).astype(jnp.int32)


def draw_pool(key, part):
    key_noise = jax.random.fold_in(key, 14)
    noise = jax.random.normal(key_noise, (POOL, PIX), jnp.float32)
    return jnp.clip(noise + drawn_rows(key), -48.0, 48.0).astype(jnp.bfloat16)


def touch_ends(result, stream_key, smallest, top_value):
    extent = result.shape
    place = [jax.random.randint(jax.random.fold_in(stream_key, axis), (), 0, extent[axis]) for axis in range(len(extent))]
    result = result.at[tuple(place)].set(smallest)
    longest = extent.index(max(extent))
    place[longest] = (place[longest] + 1) % extent[longest]
    return result.at[tuple(place)].set(top_value)


def shard_levels(key, extent, cuts, smallest, high):
    loudness, own = 1.0, jax.random.fold_in(key, 6)
    for axis_at, parts in cuts:
        heights = jnp.exp(jax.random.uniform(jax.random.fold_in(own, axis_at), (parts,), jnp.float32, smallest / len(cuts), high / len(cuts)))
        loudness = loudness * jnp.repeat(heights, extent[axis_at] // parts).reshape([-1 if axis == axis_at else 1 for axis in range(len(extent))])
    return loudness


def setup_inputs(seed: int = 0, part: int = 0) -> dict:
    key_of = jax.random.split(jax.random.key(seed), 8)
    own_keys = jax.random.split(jax.random.fold_in(key_of[7], part), 8)
    pool = draw_pool(jax.random.fold_in(jax.random.fold_in(key_of[7], part), 71), part)
    picks = draw_picks(jax.random.fold_in(jax.random.fold_in(key_of[7], part), 71), part)
    groups = touch_ends(jax.random.randint(own_keys[2], (BATCH,), 0, NGROUP), jax.random.fold_in(own_keys[2], 1), 0, NGROUP - 1).astype(jnp.int32)
    ctf_table = jnp.clip(jnp.exp(jax.random.uniform(own_keys[3], (NGROUP, CYCLES), jnp.float32, math.log(0.5), math.log(1.0))), 0.5, 1.0)
    shifts = draw_shifts(jax.random.fold_in(jax.random.fold_in(key_of[7], part), 71), part)
    classes = draw_classes(jax.random.fold_in(jax.random.fold_in(key_of[7], part), 71), part)
    log_prior = jnp.clip(jax.random.uniform(own_keys[6], (K,), jnp.float32, -1.0, 1.0) * shard_levels(own_keys[6], (K,), ((0, 4),), -0.4, 0.0), -1.0, 1.0)
    return dict(pool=pool, picks=picks, groups=groups, ctf_table=ctf_table, shifts=shifts, classes=classes, log_prior=log_prior)


STEP_WEIGHT = 0.5
PRIOR_WEIGHT = 1.0


def unrotate(images, shift_row):
    count_rows = images.shape[0]
    polar_grid = images.reshape(count_rows, CYCLES, ANG)
    doubled = jnp.concatenate([polar_grid, polar_grid], axis=2)

    def single(offset):
        return lax.dynamic_slice_in_dim(doubled, offset.astype(jnp.int32), ANG, 2).reshape(count_rows, CYCLES * ANG)

    return jax.vmap(single)(shift_row)


def all_scores(batch_rows, refs, shift_blocks):
    def single(shift_row):
        turned = unrotate(batch_rows, shift_row)
        return jnp.einsum("rnp,kp->nrk", turned.astype(jnp.float32), refs.astype(jnp.float32))

    partial_value = lax.map(single, shift_blocks)
    return jnp.transpose(partial_value, (1, 0, 2, 3)).reshape(batch_rows.shape[0], -1, refs.shape[0])


def class_numerator(batch_rows, weights, shift_blocks):
    count_rows = batch_rows.shape[0]
    nblocks, block_len = shift_blocks.shape
    classes_here = weights.shape[2]
    weight_blocks = jnp.transpose(weights.reshape(count_rows, nblocks, block_len, classes_here), (1, 0, 2, 3))

    def advance(carried, pieces):
        shift_row, weight_block = pieces
        turned = unrotate(batch_rows, shift_row)
        return carried + jnp.einsum("nrk,rnp->kp", weight_block.astype(jnp.float32), turned.astype(jnp.float32)), None

    start_value = jnp.zeros((classes_here, batch_rows.shape[1]), jnp.float32)
    numerator, _ = lax.scan(advance, start_value, (shift_blocks, weight_blocks))
    return numerator


def reference(pool, picks, groups, ctf_table, shifts, classes, log_prior):
    owner = (jnp.arange(BATCH, dtype=jnp.int32) // BATCH_DEV) * POOL_DEV
    chosen = pool[(owner + picks).astype(jnp.int32)]
    ctf_rows = ctf_table[groups]
    weighted = (chosen.astype(jnp.float32).reshape(BATCH, CYCLES, ANG) * ctf_rows[:, :, None]).reshape(BATCH, PIX).astype(jnp.bfloat16)
    ctf_sq = (ctf_rows * ctf_rows).astype(jnp.bfloat16)
    refs = classes.astype(jnp.bfloat16)
    cycle_power = jnp.sum(jnp.square(refs.astype(jnp.float32)).reshape(K, CYCLES, ANG), axis=2)
    block_len = math.gcd(ROT, 6)
    shift_blocks = shifts.reshape(ROT // block_len, block_len)
    group_rows = BATCH_DEV * N_CLS
    group_count = BATCH // group_rows

    def advance(carried, pieces):
        numerator, denominator = carried
        batch_rows, batch_sq = pieces
        scores = all_scores(batch_rows, refs, shift_blocks)
        norm_term = jnp.dot(batch_sq.astype(jnp.float32), cycle_power.T, precision=lax.Precision.HIGHEST)
        logits = scores - 0.5 * norm_term[:, None, :] + log_prior[None, None, :]
        row_top = jnp.max(logits, axis=(1, 2))
        exp_terms = jnp.exp(logits - row_top[:, None, None])
        row_total = jnp.sum(exp_terms, axis=(1, 2))
        weights = (exp_terms / row_total[:, None, None]).astype(jnp.bfloat16)
        numerator = numerator + class_numerator(batch_rows, weights, shift_blocks)
        weight_sum = jnp.sum(weights.astype(jnp.float32), axis=1)
        denominator = denominator + jnp.dot(weight_sum.T, batch_sq.astype(jnp.float32), precision=lax.Precision.HIGHEST)
        return (numerator, denominator), row_top + jnp.log(row_total)

    start_value = (jnp.zeros((K, PIX), jnp.float32), jnp.zeros((K, CYCLES), jnp.float32))
    (numerator, denominator), evidence = lax.scan(advance, start_value, (weighted.reshape(group_count, group_rows, PIX), ctf_sq.reshape(group_count, group_rows, CYCLES)))
    spread = jnp.repeat(denominator, ANG, axis=1)
    updated = (1.0 - STEP_WEIGHT) * classes + STEP_WEIGHT * numerator / (spread + PRIOR_WEIGHT)
    return (updated, evidence.reshape(BATCH))
```

```python
import functools
import math

import jax
import jax.numpy as jnp
from jax import lax
from jax.experimental import pallas as pl
from jax.experimental.pallas import tpu as pltpu
from jax.sharding import PartitionSpec as P

CYCLES = 32
ANG = 128
ROT = 36
PIX = CYCLES * ANG

STEP_WEIGHT = 0.5
PRIOR_WEIGHT = 1.0

VMEM = pl.BlockSpec(memory_space=pltpu.VMEM)
SMEM = pl.BlockSpec(memory_space=pltpu.SMEM)
F32 = jnp.float32
BF16 = jnp.bfloat16
NT = (((1,), (1,)), ((), ()))
TN = (((0,), (0,)), ((), ()))
EXACT = lax.Precision.HIGHEST
NEGATIVE = -1e30
CHUNKS = 4


def halves(total):
    high = total // 2 // 8 * 8
    width = -(-(total - high) // 8) * 8
    return high, (high + width) // 2, width


def params():
    return pltpu.CompilerParams(vmem_limit_bytes=58 * 2**20)


def weigh_kernel(picks, groups, pool, table, out):
    count, stored, ngroup = picks.shape[1], pool.shape[0], table.shape[0]
    pick_hot = (lax.broadcasted_iota(jnp.int32, (stored, count), 0) == picks[...]).astype(F32)
    group_hot = (lax.broadcasted_iota(jnp.int32, (ngroup, count), 0) == groups[...]).astype(F32)
    ctf = lax.dot_general(group_hot, table[...], TN, precision=EXACT, preferred_element_type=F32)
    chosen = lax.dot_general(pick_hot.astype(BF16), pool[...], TN, preferred_element_type=F32)
    for c in range(CYCLES):
        here = slice(c * ANG, (c + 1) * ANG)
        out[:, here] = (chosen[:, here] * ctf[:, c : c + 1]).astype(BF16)
    out[:, PIX:] = jnp.concatenate(
        [ctf * ctf, jnp.zeros((count, ANG - CYCLES), F32)], axis=1
    ).astype(BF16)


def weigh(picks, groups, pool, table):
    count = picks.shape[0]
    return pl.pallas_call(
        weigh_kernel,
        out_shape=jax.ShapeDtypeStruct((count, PIX + ANG), BF16),
        in_specs=[VMEM] * 4,
        out_specs=VMEM,
        compiler_params=params(),
        name="weigh",
    )(picks.reshape(1, -1), groups.reshape(1, -1), pool, table)


def rotate_kernel(width, place, shifts, classes, out, power):
    total = classes.shape[0]
    start, _, _ = halves(total)
    upper = place[0] == 1
    pad = jnp.zeros((width - (total - start), ANG), F32)
    lane = lax.broadcasted_iota(jnp.int32, (width, ANG), 1)

    def cycle(c, kept):
        here = pl.ds(pl.multiple_of(c * ANG, ANG), ANG)
        low = classes[0:width, here]
        high = jnp.concatenate([classes[start:total, here], pad], axis=0)
        refs = jnp.where(upper, high, low).astype(BF16).astype(F32)
        for r in range(0, ROT, 2):
            pair = [pltpu.roll(refs, shifts[r + j], 1) for j in range(2)]
            out[r * width : (r + 2) * width, here] = jnp.concatenate(pair, axis=0).astype(BF16)
        return jnp.where(lane == c, jnp.sum(refs * refs, axis=1, keepdims=True), kept)

    power[...] = lax.fori_loop(0, CYCLES, cycle, jnp.zeros((width, ANG), F32))


def rotate(width, place, shifts, classes):
    return pl.pallas_call(
        functools.partial(rotate_kernel, width),
        out_shape=(
            jax.ShapeDtypeStruct((ROT * width, PIX), BF16),
            jax.ShapeDtypeStruct((width, ANG), F32),
        ),
        in_specs=[SMEM, SMEM, VMEM],
        out_specs=(VMEM, VMEM),
        compiler_params=params(),
        name="rotate",
    )(place, shifts, classes)


def score_kernel(width, steps, place, turned, images, power, prior, logits, stats):
    step = pl.program_id(0)
    rows = turned.shape[0]
    count = images.shape[0]
    squares = images[:, PIX : PIX + ANG].astype(F32)
    norm = lax.dot_general(power[...], squares, NT, precision=EXACT, preferred_element_type=F32)
    total = prior.shape[0]
    start, cut, _ = halves(total)
    upper = place[0] == 1
    row = lax.broadcasted_iota(jnp.int32, norm.shape, 0)
    pad = jnp.zeros((width - (total - start), 1), F32)
    high = jnp.concatenate([prior[start:total, :], pad], axis=0)
    mine = (row >= jnp.where(upper, cut - start, 0)) & (row < jnp.where(upper, total - start, cut))
    bias = jnp.where(mine, jnp.where(upper, high, prior[0:width, :]) - 0.5 * norm, NEGATIVE)
    scores = lax.dot_general(turned[...], images[:, :PIX], NT, preferred_element_type=F32)
    for j in range(rows // width):
        block = pl.ds(pl.multiple_of(step * rows + j * width, 8), width)
        logits[block, :] = scores[j * width : (j + 1) * width, :] + bias

    @pl.when(step == steps - 1)
    def _():
        def highest(r, top):
            return jnp.maximum(top, logits[pl.ds(pl.multiple_of(r * width, 8), width), :])

        top = lax.fori_loop(1, ROT, highest, logits[0:width, :])
        top = jnp.max(top, axis=0, keepdims=True)

        def add(r, total):
            return total + jnp.exp(logits[pl.ds(pl.multiple_of(r * width, 8), width), :] - top)

        total = lax.fori_loop(0, ROT, add, jnp.zeros((width, count), F32))
        stats[0:1, :] = top
        stats[1:2, :] = jnp.sum(total, axis=0, keepdims=True)
        stats[2:8, :] = jnp.zeros((6, count), F32)


def score(width, place, turned, images, power, prior):
    steps = 4
    rows = ROT * width // steps
    count = images.shape[0]
    whole = lambda i: (0, 0)
    return pl.pallas_call(
        functools.partial(score_kernel, width, steps),
        grid=(steps,),
        out_shape=(
            jax.ShapeDtypeStruct((ROT * width, count), F32),
            jax.ShapeDtypeStruct((8, count), F32),
        ),
        in_specs=[
            SMEM,
            pl.BlockSpec((rows, PIX), lambda i: (i, 0)),
            pl.BlockSpec(images.shape, whole),
            pl.BlockSpec(power.shape, whole),
            pl.BlockSpec(prior.shape, whole),
        ],
        out_specs=(
            pl.BlockSpec((ROT * width, count), whole),
            pl.BlockSpec((8, count), whole),
        ),
        compiler_params=params(),
        name="score",
    )(place, turned, images, power, prior)


def weight_kernel(width, place, logits, squares, *refs):
    stats, (weights, evidence, inverse, joined) = refs[:-4], refs[-4:]
    count = logits.shape[1]
    me = place[1]
    for m, stat in enumerate(stats):
        joined[pl.ds(pl.multiple_of((me ^ m) * 8, 8), 8), :] = stat[...]
    tops = [joined[8 * j : 8 * j + 1, :] for j in range(len(stats))]
    totals = [joined[8 * j + 1 : 8 * j + 2, :] for j in range(len(stats))]
    top = functools.reduce(jnp.maximum, tops)
    total = sum(t * jnp.exp(h - top) for h, t in zip(tops, totals))
    evidence[...] = jnp.broadcast_to(top + jnp.log(total), (8, count))
    scale = 1.0 / total

    def single(q, summed):
        values = []
        for j in range(2):
            block = pl.ds(pl.multiple_of((2 * q + j) * width, 8), width)
            values.append((jnp.exp(logits[block, :] - top) * scale))
        pair = jnp.concatenate(values, axis=0).astype(BF16)
        weights[pl.ds(pl.multiple_of(2 * q * width, 16), 2 * width), :] = pair
        pair = pair.astype(F32)
        return summed + (pair[:width] + pair[width:])

    summed = lax.fori_loop(0, ROT // 2, single, jnp.zeros((width, count), F32))
    denominator = jnp.dot(
        summed, squares[...].astype(F32), precision=EXACT, preferred_element_type=F32
    )
    inverse[...] = 1.0 / (denominator + PRIOR_WEIGHT)


def weigh_classes(width, place, logits, images, stats):
    count = logits.shape[1]
    squares = pl.BlockSpec((count, ANG), lambda i: (0, PIX // ANG))
    whole = lambda a: pl.BlockSpec(a.shape, lambda i: (0, 0))
    outs = (
        jax.ShapeDtypeStruct((ROT * width, count), BF16),
        jax.ShapeDtypeStruct((8, count), F32),
        jax.ShapeDtypeStruct((width, ANG), F32),
    )
    return pl.pallas_call(
        functools.partial(weight_kernel, width),
        grid=(1,),
        out_shape=outs,
        in_specs=[SMEM, whole(logits), squares] + [whole(s) for s in stats],
        out_specs=tuple(whole(o) for o in outs),
        scratch_shapes=[pltpu.VMEM((8 * len(stats), count), F32)],
        compiler_params=params(),
        name="weights",
    )(place, logits, images, *stats)


def update_kernel(width, first, span, shifts, weights, images, inverse, out, product):
    step = pl.program_id(0)
    product[...] = jnp.dot(weights[...], images[...], preferred_element_type=F32)
    lane = lax.broadcasted_iota(jnp.int32, (width, ANG), 1)
    for j in range(span):
        here = slice(j * ANG, (j + 1) * ANG)
        total = jnp.zeros((width, ANG), F32)
        for r in range(ROT):
            total = total + pltpu.roll(
                product[r * width : (r + 1) * width, here], (ANG - shifts[r]) & (ANG - 1), 1
            )
        cycle = first + step * span + j
        share = jnp.sum(jnp.where(lane == cycle, inverse[...], 0.0), axis=1, keepdims=True)
        out[:, here] = (total * share).astype(BF16)


def update(width, part, parts, shifts, weights, images, inverse):
    count = images.shape[0]
    cycles = CYCLES // parts
    span = 2
    steps = cycles // span
    whole = lambda i: (0, 0)
    return pl.pallas_call(
        functools.partial(update_kernel, width, part * cycles, span),
        grid=(steps,),
        out_shape=jax.ShapeDtypeStruct((width, cycles * ANG), BF16),
        in_specs=[
            SMEM,
            pl.BlockSpec(weights.shape, whole),
            pl.BlockSpec((count, span * ANG), lambda i: (0, part * steps + i)),
            pl.BlockSpec(inverse.shape, whole),
        ],
        out_specs=pl.BlockSpec((width, span * ANG), lambda i: (0, i)),
        scratch_shapes=[pltpu.VMEM((ROT * width, span * ANG), F32)],
        compiler_params=params(),
        name="update",
    )(shifts, weights, images, inverse)


def blend_kernel(width, place, classes, *refs):
    out = refs[-1]
    parts = (len(refs) - 1) // 2
    total = classes.shape[0]
    start, cut, _ = halves(total)
    upper = place[0] == 1
    span = PIX // parts
    row = lax.broadcasted_iota(jnp.int32, (total, span), 0)
    for p in range(parts):
        here = slice(p * span, (p + 1) * span)
        mine, other = refs[p][...].astype(F32), refs[parts + p][...].astype(F32)
        low = jnp.where(upper, other, mine)
        high = jnp.where(upper, mine, other)
        low_all = jnp.concatenate([low, jnp.zeros((total - width, span), F32)], axis=0)
        high_all = jnp.concatenate([jnp.zeros((start, span), F32), high[: total - start]], axis=0)
        step = jnp.where(row < cut, low_all, high_all)
        out[:, here] = (1.0 - STEP_WEIGHT) * classes[:, here] + STEP_WEIGHT * step


def blend(width, place, classes, mine, other):
    return pl.pallas_call(
        functools.partial(blend_kernel, width),
        out_shape=jax.ShapeDtypeStruct(classes.shape, F32),
        in_specs=[SMEM] + [VMEM] * (1 + 2 * len(mine)),
        out_specs=VMEM,
        compiler_params=params(),
        name="blend",
    )(place, classes, *mine, *other)


def halved(pool, picks, groups, ctf_table, shifts, classes, log_prior):
    _, _, width = halves(classes.shape[0])
    axes = ("particle", "cls")
    n_cls = lax.axis_size("cls")
    z, cls = lax.axis_index("particle"), lax.axis_index("cls")
    half = jnp.where((z == 0) | (z == 3), 0, 1).astype(jnp.int32)
    place = jnp.stack([half, half * n_cls + cls, z]).astype(jnp.int32)
    own = weigh(picks, groups, pool, ctf_table)
    images = lax.all_gather(own, axes, axis=0, tiled=True)
    turned, power = rotate(width, place, shifts, classes)
    logits, stat = score(width, place, turned, images, power, log_prior.reshape(-1, 1))
    n_all = lax.axis_size("particle") * n_cls
    stats = [stat] + [
        lax.ppermute(stat, axes, [(i, i ^ m) for i in range(n_all)]) for m in range(1, 2 * n_cls)
    ]
    weights, evidence, inverse = weigh_classes(width, place, logits, images, stats)
    mine = [
        update(width, p, CHUNKS, shifts, weights, images, inverse) for p in range(CHUNKS)
    ]
    swap = [(i, i ^ 1) for i in range(lax.axis_size("particle"))]
    other = [lax.ppermute(u, "particle", swap) for u in mine]
    updated = blend(width, place, classes, mine, other)
    count = picks.shape[0] * n_cls
    log_evidence = lax.dynamic_slice(evidence, (0, z * count), (1, count)).reshape(count)
    return (updated, log_evidence)


def joined(part, axis, combine):
    gathered = jax.tree.map(lambda a: lax.all_gather(a, axis), part)

    def take(source):
        return jax.tree.map(lambda a: lax.dynamic_index_in_dim(a, source, 0, False), gathered)

    return lax.fori_loop(
        1, lax.axis_size(axis), lambda source, state: combine(state, take(source)), take(0)
    )


def angle_major(images):
    count_rows = images.shape[0]
    return jnp.transpose(images.reshape(count_rows, CYCLES, ANG), (2, 1, 0)).reshape(
        ANG * CYCLES, count_rows
    )


def turned_view(doubled, offset):
    return lax.dynamic_slice_in_dim(doubled, offset * CYCLES, ANG * CYCLES, 0)


def all_scores(doubled, refs_major, shift_blocks):
    block_len = shift_blocks.shape[1]

    def single(shift_row):
        outputs = []
        for slot in range(block_len):
            piece = turned_view(doubled, shift_row[slot])
            outputs.append(
                lax.dot_general(
                    piece, refs_major, (((0,), (0,)), ((), ())), preferred_element_type=jnp.float32
                )
            )
        return jnp.stack(outputs, axis=0)

    partial_value = lax.map(single, shift_blocks)
    return partial_value.reshape(-1, partial_value.shape[2], partial_value.shape[3])


def class_numerator(doubled, weights, shift_blocks):
    nblocks, block_len = shift_blocks.shape
    weight_blocks = weights.reshape(nblocks, block_len, weights.shape[1], weights.shape[2])

    def advance(carried, pieces):
        shift_row, weight_block = pieces
        for slot in range(block_len):
            piece = turned_view(doubled, shift_row[slot])
            carried = carried + jnp.dot(
                piece, weight_block[slot], preferred_element_type=jnp.float32
            )
        return (carried, None)

    start_value = jnp.zeros((ANG * CYCLES, weights.shape[2]), jnp.float32)
    numerator_major, _ = lax.scan(advance, start_value, (shift_blocks, weight_blocks))
    classes_here = weights.shape[2]
    return jnp.transpose(numerator_major.reshape(ANG, CYCLES, classes_here), (2, 1, 0)).reshape(
        classes_here, CYCLES * ANG
    )


def merge_softmax(earlier, later):
    row_top = jnp.maximum(earlier[0], later[0])
    row_total = earlier[1] * jnp.exp(earlier[0] - row_top) + later[1] * jnp.exp(later[0] - row_top)
    return (row_top, row_total)


def whole_sum(pool, picks, groups, ctf_table, shifts, classes, log_prior):
    chosen = jnp.take(pool, picks, axis=0)
    count_local = chosen.shape[0]
    onehot_rows = (
        groups[:, None] == jnp.arange(ctf_table.shape[0], dtype=jnp.int32)[None, :]
    ).astype(jnp.float32)
    ctf_rows = jnp.dot(onehot_rows, ctf_table, precision=lax.Precision.HIGHEST)
    weighted = (
        (chosen.astype(jnp.float32).reshape(count_local, CYCLES, ANG) * ctf_rows[:, :, None])
        .reshape(count_local, CYCLES * ANG)
        .astype(jnp.bfloat16)
    )
    ctf_sq = (ctf_rows * ctf_rows).astype(jnp.bfloat16)
    batch_rows, batch_sq = (
        lax.all_gather(weighted, "cls", axis=0, tiled=True),
        lax.all_gather(ctf_sq, "cls", axis=0, tiled=True),
    )
    batch_major = angle_major(batch_rows)
    doubled = jnp.concatenate([batch_major, batch_major], axis=0)
    refs = classes.astype(jnp.bfloat16)
    refs_major = angle_major(refs)
    cycle_power = jnp.sum(
        jnp.square(refs.astype(jnp.float32)).reshape(classes.shape[0], CYCLES, ANG), axis=2
    )
    block_len = math.gcd(ROT, 6)
    shift_blocks = shifts.reshape(ROT // block_len, block_len)
    scores = all_scores(doubled, refs_major, shift_blocks)
    norm_term = jnp.dot(
        batch_sq.astype(jnp.float32), cycle_power.T, precision=lax.Precision.HIGHEST
    )
    logits = scores - 0.5 * norm_term[None, :, :] + log_prior[None, None, :]
    local_top = jnp.max(logits, axis=(0, 2))
    local_total = jnp.sum(jnp.exp(logits - local_top[None, :, None]), axis=(0, 2))
    row_top, row_total = joined((local_top, local_total), "cls", merge_softmax)
    exp_terms = jnp.exp(logits - row_top[None, :, None])
    weights = (exp_terms / row_total[None, :, None]).astype(jnp.bfloat16)
    log_evidence = row_top + jnp.log(row_total)
    numerator = class_numerator(doubled, weights, shift_blocks)
    weight_sum = jnp.sum(weights.astype(jnp.float32), axis=0)
    denominator = lax.dot_general(
        weight_sum,
        batch_sq.astype(jnp.float32),
        (((0,), (0,)), ((), ())),
        precision=lax.Precision.HIGHEST,
    )
    numerator, denominator = lax.psum((numerator, denominator), "particle")
    spread = jnp.repeat(denominator, ANG, axis=1)
    updated = (1.0 - STEP_WEIGHT) * classes + STEP_WEIGHT * numerator / (spread + PRIOR_WEIGHT)
    return (updated, log_evidence)


def solution(mesh):
    in_specs = (
        P(("groups", "particle", "cls"), None),
        P(("groups", "particle", "cls")),
        P(("groups", "particle", "cls")),
        P("groups", None),
        P("groups"),
        P(("groups", "cls"), None),
        P(("groups", "cls")),
    )
    out_specs = (P(("groups", "cls"), None), P(("groups", "particle")))
    quad = mesh.shape["particle"] == 4 and mesh.shape["cls"] == 4
    return jax.shard_map(
        halved if quad else whole_sum, mesh=mesh, in_specs=in_specs, out_specs=out_specs, check_vma=False
    )
```

```python
import functools
import math

import jax
import jax.numpy as jnp
from jax import lax
from jax.experimental import pallas as pl
from jax.experimental.pallas import tpu as pltpu
from jax.sharding import PartitionSpec as P

CYCLES = 32
ANG = 128
ROT = 36
PIX = CYCLES * ANG

STEP_WEIGHT = 0.5
PRIOR_WEIGHT = 1.0

VMEM = pl.BlockSpec(memory_space=pltpu.VMEM)
ANY = pl.BlockSpec(memory_space=pl.ANY)
SMEM = pl.BlockSpec(memory_space=pltpu.SMEM)
F32 = jnp.float32
BF16 = jnp.bfloat16
NT = (((1,), (1,)), ((), ()))
TN = (((0,), (0,)), ((), ()))
EXACT = lax.Precision.HIGHEST
NEGATIVE = -1e30
CHUNKS = (8, 8, 8, 8)
LARGE = 48


def later(kernel, count):
    return lambda *refs: kernel(*refs[count:])


def halves(total):
    start = total // 2 // 8 * 8
    rows = -(-(total - start) // 8) * 8
    return start, (start + rows) // 2, rows, -(-rows // 16) * 16


def cost(flops, moved):
    return pl.CostEstimate(flops=int(flops), bytes_accessed=int(moved), transcendentals=0)


def params(mib=8):
    return pltpu.CompilerParams(vmem_limit_bytes=mib * 2**20)


def weigh_kernel(picks, groups, pool, table, out):
    count, stored, ngroup = picks.shape[1], pool.shape[0], table.shape[1]
    pick_hot = (lax.broadcasted_iota(jnp.int32, (stored, count), 0) == picks[...]).astype(F32)
    group_hot = (lax.broadcasted_iota(jnp.int32, (ngroup, count), 0) == groups[...]).astype(F32)
    ctf = jnp.dot(table[...], group_hot, precision=EXACT, preferred_element_type=F32).T
    chosen = lax.dot_general(pick_hot.astype(BF16), pool[...], TN, preferred_element_type=F32)
    for c in range(CYCLES):
        here = slice(c * ANG, (c + 1) * ANG)
        out[:, here] = (chosen[:, here] * ctf[:, c : c + 1]).astype(BF16)
    out[:, PIX:] = jnp.concatenate(
        [ctf * ctf, jnp.zeros((count, ANG - CYCLES), F32)], axis=1
    ).astype(BF16)


def weigh(picks, groups, pool, table):
    count = picks.shape[0]
    return pl.pallas_call(
        weigh_kernel,
        out_shape=jax.ShapeDtypeStruct((count, PIX + ANG), BF16),
        in_specs=[VMEM] * 4,
        out_specs=VMEM,
        compiler_params=params(),
        cost_estimate=cost(2 * count * 48 * PIX, 2**20),
        name="weigh",
    )(picks.reshape(1, -1), groups.reshape(1, -1), pool, table.T)


def score_kernel(width, groups, span, place, shifts, prior, classes, same, across, *refs):
    (logits, stats, images), (halved, bias, *turned) = refs[:3], refs[3:]
    one = same.shape[0]
    count = images.shape[0]
    core = place[2]
    upper = place[0] == 1
    total = classes.shape[0]
    start, cut, _, _ = halves(total)
    images[pl.ds(pl.multiple_of(core * one, 16), one), :] = same[...]
    images[pl.ds(pl.multiple_of((1 - core) * one, 16), one), :] = across[...]

    pad = jnp.zeros((width - (total - start), ANG), F32)
    lane = lax.broadcasted_iota(jnp.int32, (width, ANG), 1)
    power = jnp.zeros((width, ANG), F32)
    for c in range(CYCLES):
        here = slice(c * ANG, (c + 1) * ANG)
        high = jnp.concatenate([classes[start:total, here], pad], axis=0)
        mine = jnp.where(upper, high, classes[0:width, here]).astype(BF16)
        halved[:, here] = mine
        wide = mine.astype(F32)
        power = jnp.where(lane == c, jnp.sum(wide * wide, axis=1, keepdims=True), power)

    squares = images[:, PIX:].astype(F32)
    norm = lax.dot_general(power, squares, NT, precision=EXACT, preferred_element_type=F32)
    column = jnp.broadcast_to(prior[...], (8, ANG)).T[:, 0:1]
    high = jnp.concatenate([column[start:total, :], pad[:, 0:1]], axis=0)
    value = jnp.where(upper, high, column[0:width, :]) - 0.5 * norm
    row = lax.broadcasted_iota(jnp.int32, norm.shape, 0)
    mine = (row >= jnp.where(upper, cut - start, 0)) & (
        row < jnp.where(upper, total - start, cut)
    )
    bias[...] = jnp.where(mine, value, NEGATIVE)

    each = ROT // groups
    top = jnp.full((width, count), NEGATIVE, F32)
    for g in range(groups):
        scores = None
        for q in range(CYCLES // span):
            block = turned[q % 2]
            for c in range(span):
                cycle = q * span + c
                image = halved[:, cycle * ANG : (cycle + 1) * ANG]
                for r in range(each):
                    block[r * width : (r + 1) * width, c * ANG : (c + 1) * ANG] = pltpu.roll(
                        image, shifts[g * each + r], 1
                    )
            part = lax.dot_general(
                block[...],
                images[:, q * span * ANG : (q + 1) * span * ANG],
                NT,
                preferred_element_type=F32,
            )
            scores = part if scores is None else scores + part
        for r in range(each):
            value = scores[r * width : (r + 1) * width, :] + bias[...]
            logits[(g * each + r) * width : (g * each + r + 1) * width, :] = value
            top = jnp.maximum(top, value)
    top = jnp.max(top, axis=0, keepdims=True)

    def add(r, total):
        return total + jnp.exp(logits[pl.ds(pl.multiple_of(r * width, 8), width), :] - top)

    total = lax.fori_loop(0, ROT, add, jnp.zeros((width, count), F32))
    stats[0:1, :] = top
    stats[1:2, :] = jnp.sum(total, axis=0, keepdims=True)
    stats[2:, :] = jnp.zeros((6, count), F32)


def score(width, place, shifts, prior, classes, same, across):
    groups, span = 4, 4
    one, full = same.shape
    count = 2 * one
    outs = (
        jax.ShapeDtypeStruct((ROT * width, count), F32),
        jax.ShapeDtypeStruct((8, count), F32),
        jax.ShapeDtypeStruct((count, full), BF16),
    )
    return pl.pallas_call(
        functools.partial(score_kernel, width, groups, span),
        out_shape=outs,
        in_specs=[SMEM, SMEM] + [VMEM] * 4,
        out_specs=(VMEM,) * 3,
        scratch_shapes=[pltpu.VMEM((width, PIX), BF16), pltpu.VMEM((width, count), F32)]
        + [pltpu.VMEM((ROT // groups * width, span * ANG), BF16)] * 2,
        compiler_params=params(LARGE),
        cost_estimate=cost(10 * 2**30, 20 * 2**20),
        name="score",
    )(place, shifts, prior, classes, same, across)


def weight_kernel(width, place, logits, squares, *refs):
    stats, (weights, evidence, denominator, joined) = refs[:-4], refs[-4:]
    count = logits.shape[1]
    for m, stat in enumerate(stats):
        joined[pl.ds(pl.multiple_of((place[1] ^ m) * 8, 8), 8), :] = stat[...]
    tops = [joined[8 * j : 8 * j + 1, :] for j in range(len(stats))]
    totals = [joined[8 * j + 1 : 8 * j + 2, :] for j in range(len(stats))]
    top = functools.reduce(jnp.maximum, tops)
    total = sum(t * jnp.exp(h - top) for h, t in zip(tops, totals))
    evidence[...] = jnp.broadcast_to(top + jnp.log(total), (8, count))
    scale = 1.0 / total

    def single(r, summed):
        block = pl.ds(pl.multiple_of(r * width, 16), width)
        value = (jnp.exp(logits[block, :] - top) * scale).astype(BF16)
        weights[block, :] = value
        return summed + value.astype(F32)

    summed = lax.fori_loop(0, ROT, single, jnp.zeros((width, count), F32))
    denominator[...] = jnp.dot(
        summed, squares[...].astype(F32), precision=EXACT, preferred_element_type=F32
    )


def weigh_classes(width, place, logits, images, stats):
    count = logits.shape[1]
    squares = pl.BlockSpec((count, ANG), lambda i: (0, PIX // ANG))
    whole = lambda a: pl.BlockSpec(a.shape, lambda i: (0, 0))
    outs = (
        jax.ShapeDtypeStruct((ROT * width, count), BF16),
        jax.ShapeDtypeStruct((8, count), F32),
        jax.ShapeDtypeStruct((width, ANG), F32),
    )
    return pl.pallas_call(
        functools.partial(weight_kernel, width),
        grid=(1,),
        out_shape=outs,
        in_specs=[SMEM, whole(logits), squares] + [whole(s) for s in stats],
        out_specs=tuple(whole(o) for o in outs),
        scratch_shapes=[pltpu.VMEM((8 * len(stats), count), F32)],
        compiler_params=params(LARGE),
        cost_estimate=cost(4 * 2**30, 8 * 2**20),
        name="weights",
    )(place, logits, images, *stats)


def update_kernel(width, rows, span, shifts, weights, images, out, product):
    product[...] = jnp.dot(weights[...], images[...], preferred_element_type=F32).astype(BF16)
    for j in range(span):
        here = slice(j * ANG, (j + 1) * ANG)
        total = jnp.zeros((width, ANG), F32)
        for r in range(ROT):
            back = (ANG - shifts[r]) & (ANG - 1)
            turned = pltpu.roll(product[r * width : (r + 1) * width, here], back, 1)
            total = total + turned.astype(F32)
        out[:, here] = total[:rows].astype(BF16)


def update(width, rows, first, cycles, shifts, weights, images, after):
    count = images.shape[0]
    span = math.gcd(cycles, 8)
    base = first // span
    return pl.pallas_call(
        later(functools.partial(update_kernel, width, rows, span), len(after)),
        grid=(cycles // span,),
        out_shape=jax.ShapeDtypeStruct((rows, cycles * ANG), BF16),
        in_specs=[ANY] * len(after)
        + [
            SMEM,
            pl.BlockSpec(weights.shape, lambda i: (0, 0)),
            pl.BlockSpec((count, span * ANG), lambda i: (0, base + i)),
        ],
        out_specs=pl.BlockSpec((rows, span * ANG), lambda i: (0, i)),
        scratch_shapes=[pltpu.VMEM((ROT * width, span * ANG), BF16)],
        compiler_params=params(LARGE),
        cost_estimate=cost(3 * 2**30, 4 * 2**20),
        name="update",
    )(*after, shifts, weights, images)


def divide_kernel(first, one, two, one_below, two_below, out):
    rows, span = out.shape
    below = one_below[0:rows, :] + two_below[0:rows, :]
    share = 1.0 / (below + PRIOR_WEIGHT)
    lane = lax.broadcasted_iota(jnp.int32, share.shape, 1)
    for j in range(span // ANG):
        here = slice(j * ANG, (j + 1) * ANG)
        total = one[:, here].astype(F32) + two[:, here].astype(F32)
        cycle = jnp.where(lane == first + j, share, 0.0)
        out[:, here] = (total * jnp.sum(cycle, axis=1, keepdims=True)).astype(BF16)


def divide(first, one, two, one_below, two_below):
    return pl.pallas_call(
        functools.partial(divide_kernel, first),
        out_shape=jax.ShapeDtypeStruct(one.shape, BF16),
        in_specs=[VMEM] * 4,
        out_specs=VMEM,
        compiler_params=params(8),
        cost_estimate=cost(2**30, 2**20),
        name="divide",
    )(one, two, one_below, two_below)


def blend_kernel(place, classes, mine, other, *refs):
    out = refs[-1]
    total, span = classes.shape
    width = mine.shape[0]
    start, cut, _, _ = halves(total)
    upper = place[0] == 1
    row = lax.broadcasted_iota(jnp.int32, (total, span), 0)
    first, second = mine[...].astype(F32), other[...].astype(F32)
    low = jnp.where(upper, second, first)
    high = jnp.where(upper, first, second)
    low_all = jnp.concatenate([low, jnp.zeros((total - width, span), F32)], axis=0)
    high_all = jnp.concatenate([jnp.zeros((start, span), F32), high[: total - start]], axis=0)
    step = jnp.where(row < cut, low_all, high_all)
    out[...] = (1.0 - STEP_WEIGHT) * classes[...] + STEP_WEIGHT * step


def blend(first, place, classes, mine, other, before):
    span = mine.shape[1]
    rows = pl.BlockSpec((classes.shape[0], span), lambda i: (0, first * ANG // span))
    update = pl.BlockSpec(mine.shape, lambda i: (0, 0))
    return pl.pallas_call(
        blend_kernel,
        grid=(1,),
        out_shape=jax.ShapeDtypeStruct(classes.shape, F32),
        in_specs=[SMEM, rows, update, update] + [ANY] * len(before),
        out_specs=rows,
        input_output_aliases={4: 0} if before else {},
        compiler_params=params(),
        cost_estimate=cost(2**30, 2**20),
        name="blend",
    )(place, classes, mine, other, *before)


def halved(pool, picks, groups, ctf_table, shifts, classes, log_prior):
    total = classes.shape[0]
    _, _, rows, width = halves(total)
    axes = ("particle", "cls")
    z, cls = lax.axis_index("particle"), lax.axis_index("cls")
    chip, core = cls // 2, cls % 2
    half = jnp.where((z == 1) | (z == 2), 1, 0)
    place = jnp.stack([half, half * 2 + chip, core]).astype(jnp.int32)
    prior = jnp.pad(log_prior, (0, ANG - total)).reshape(1, ANG)

    def swap(a, mask):
        return lax.ppermute(a, axes, [(i, i ^ mask) for i in range(16)])

    CORE, CHIP, NEXT, SAME = 1, 2, 4, 12

    own = weigh(picks, groups, pool, ctf_table)
    beside = swap(own, NEXT)
    own_x = swap(own, CHIP)
    beside_x = swap(beside, CHIP)
    pairs = [
        (jnp.where(chip == 1, x, a), jnp.where(chip == 1, a, x))
        for a, x in ((own, own_x), (beside, beside_x))
    ]
    odd = z % 2 == 1
    low = [jnp.where(odd, b, a) for a, b in zip(*pairs)]
    high = [jnp.where(odd, a, b) for a, b in zip(*pairs)]
    same = jnp.concatenate(low + high, axis=0)
    across = swap(same, CORE)

    logits, stat, images = score(width, place, shifts, prior, classes, same, across)

    stat_core = swap(stat, CORE)
    first = jnp.where(core == 0, stat, stat_core)
    second = jnp.where(core == 0, stat_core, stat)
    top = jnp.maximum(first[0], second[0])
    both = first[1] * jnp.exp(first[0] - top) + second[1] * jnp.exp(second[0] - top)
    stat = jnp.concatenate([top[None], both[None], stat[2:]], axis=0)
    stats = [stat] + [swap(stat, m) for m in (CHIP, NEXT, NEXT + CHIP)]
    weights, evidence, below = weigh_classes(width, place, logits, images, stats)
    other_below = swap(below, SAME)

    mine, other, ratios, others, firsts = [], [], [], [], []
    for p, cycles in enumerate(CHUNKS):
        firsts.append(sum(CHUNKS[:p]))
        after = tuple(mine[-1:]) + tuple(ratios[: p - 1][-1:] if p > 1 else ())
        mine.append(update(width, rows, firsts[p], cycles, shifts, weights, images, after))
        other.append(swap(mine[p], SAME))
        ratios.append(divide(firsts[p], mine[p], other[p], below, other_below))
        others.append(swap(ratios[p], NEXT))
    updated = ()
    for p in range(len(CHUNKS)):
        updated = (blend(firsts[p], place, classes, ratios[p], others[p], updated),)
    count = picks.shape[0]
    by_shard = evidence[0].reshape(2, 2, 2, count)
    log_evidence = jnp.take(by_shard, z % 2, axis=1)
    return (updated[0], jnp.transpose(log_evidence, (1, 0, 2)).reshape(4 * count))


def joined(part, axis, combine):
    gathered = jax.tree.map(lambda a: lax.all_gather(a, axis), part)

    def take(source):
        return jax.tree.map(lambda a: lax.dynamic_index_in_dim(a, source, 0, False), gathered)

    return lax.fori_loop(
        1, lax.axis_size(axis), lambda source, state: combine(state, take(source)), take(0)
    )


def angle_major(images):
    count_rows = images.shape[0]
    return jnp.transpose(images.reshape(count_rows, CYCLES, ANG), (2, 1, 0)).reshape(
        ANG * CYCLES, count_rows
    )


def turned_view(doubled, offset):
    return lax.dynamic_slice_in_dim(doubled, offset * CYCLES, ANG * CYCLES, 0)


def all_scores(doubled, refs_major, shift_blocks):
    block_len = shift_blocks.shape[1]

    def single(shift_row):
        outputs = []
        for slot in range(block_len):
            piece = turned_view(doubled, shift_row[slot])
            outputs.append(
                lax.dot_general(
                    piece, refs_major, (((0,), (0,)), ((), ())), preferred_element_type=jnp.float32
                )
            )
        return jnp.stack(outputs, axis=0)

    partial_value = lax.map(single, shift_blocks)
    return partial_value.reshape(-1, partial_value.shape[2], partial_value.shape[3])


def class_numerator(doubled, weights, shift_blocks):
    nblocks, block_len = shift_blocks.shape
    weight_blocks = weights.reshape(nblocks, block_len, weights.shape[1], weights.shape[2])

    def advance(carried, pieces):
        shift_row, weight_block = pieces
        for slot in range(block_len):
            piece = turned_view(doubled, shift_row[slot])
            carried = carried + jnp.dot(
                piece, weight_block[slot], preferred_element_type=jnp.float32
            )
        return (carried, None)

    start_value = jnp.zeros((ANG * CYCLES, weights.shape[2]), jnp.float32)
    numerator_major, _ = lax.scan(advance, start_value, (shift_blocks, weight_blocks))
    classes_here = weights.shape[2]
    return jnp.transpose(numerator_major.reshape(ANG, CYCLES, classes_here), (2, 1, 0)).reshape(
        classes_here, CYCLES * ANG
    )


def merge_softmax(earlier, later):
    row_top = jnp.maximum(earlier[0], later[0])
    row_total = earlier[1] * jnp.exp(earlier[0] - row_top) + later[1] * jnp.exp(later[0] - row_top)
    return (row_top, row_total)


def whole_sum(pool, picks, groups, ctf_table, shifts, classes, log_prior):
    chosen = jnp.take(pool, picks, axis=0)
    count_local = chosen.shape[0]
    onehot_rows = (
        groups[:, None] == jnp.arange(ctf_table.shape[0], dtype=jnp.int32)[None, :]
    ).astype(jnp.float32)
    ctf_rows = jnp.dot(onehot_rows, ctf_table, precision=lax.Precision.HIGHEST)
    weighted = (
        (chosen.astype(jnp.float32).reshape(count_local, CYCLES, ANG) * ctf_rows[:, :, None])
        .reshape(count_local, CYCLES * ANG)
        .astype(jnp.bfloat16)
    )
    ctf_sq = (ctf_rows * ctf_rows).astype(jnp.bfloat16)
    batch_rows, batch_sq = (
        lax.all_gather(weighted, "cls", axis=0, tiled=True),
        lax.all_gather(ctf_sq, "cls", axis=0, tiled=True),
    )
    batch_major = angle_major(batch_rows)
    doubled = jnp.concatenate([batch_major, batch_major], axis=0)
    refs = classes.astype(jnp.bfloat16)
    refs_major = angle_major(refs)
    cycle_power = jnp.sum(
        jnp.square(refs.astype(jnp.float32)).reshape(classes.shape[0], CYCLES, ANG), axis=2
    )
    block_len = math.gcd(ROT, 6)
    shift_blocks = shifts.reshape(ROT // block_len, block_len)
    scores = all_scores(doubled, refs_major, shift_blocks)
    norm_term = jnp.dot(
        batch_sq.astype(jnp.float32), cycle_power.T, precision=lax.Precision.HIGHEST
    )
    logits = scores - 0.5 * norm_term[None, :, :] + log_prior[None, None, :]
    local_top = jnp.max(logits, axis=(0, 2))
    local_total = jnp.sum(jnp.exp(logits - local_top[None, :, None]), axis=(0, 2))
    row_top, row_total = joined((local_top, local_total), "cls", merge_softmax)
    exp_terms = jnp.exp(logits - row_top[None, :, None])
    weights = (exp_terms / row_total[None, :, None]).astype(jnp.bfloat16)
    log_evidence = row_top + jnp.log(row_total)
    numerator = class_numerator(doubled, weights, shift_blocks)
    weight_sum = jnp.sum(weights.astype(jnp.float32), axis=0)
    denominator = lax.dot_general(
        weight_sum,
        batch_sq.astype(jnp.float32),
        (((0,), (0,)), ((), ())),
        precision=lax.Precision.HIGHEST,
    )
    numerator, denominator = lax.psum((numerator, denominator), "particle")
    spread = jnp.repeat(denominator, ANG, axis=1)
    updated = (1.0 - STEP_WEIGHT) * classes + STEP_WEIGHT * numerator / (spread + PRIOR_WEIGHT)
    return (updated, log_evidence)


def solution(mesh):
    in_specs = (
        P(("groups", "particle", "cls"), None),
        P(("groups", "particle", "cls")),
        P(("groups", "particle", "cls")),
        P("groups", None),
        P("groups"),
        P(("groups", "cls"), None),
        P(("groups", "cls")),
    )
    out_specs = (P(("groups", "cls"), None), P(("groups", "particle")))
    quad = mesh.shape["particle"] == 4 and mesh.shape["cls"] == 4
    return jax.shard_map(
        halved if quad else whole_sum, mesh=mesh, in_specs=in_specs, out_specs=out_specs, check_vma=False
    )
```

```python
import functools
import math

import jax
import jax.numpy as jnp
from jax import lax
from jax.experimental import pallas as pl
from jax.experimental.pallas import tpu as pltpu
from jax.sharding import PartitionSpec as P

CYCLES = 32
ANG = 128
ROT = 36
PIX = CYCLES * ANG

STEP_WEIGHT = 0.5
PRIOR_WEIGHT = 1.0

VMEM = pl.BlockSpec(memory_space=pltpu.VMEM)
ANY = pl.BlockSpec(memory_space=pl.ANY)
SMEM = pl.BlockSpec(memory_space=pltpu.SMEM)
F32 = jnp.float32
BF16 = jnp.bfloat16
NT = (((1,), (1,)), ((), ()))
TN = (((0,), (0,)), ((), ()))
EXACT = lax.Precision.HIGHEST
NEGATIVE = -1e30
CHUNKS = (8, 8, 8, 8)
LARGE = 58


def later(kernel, count):
    return lambda *refs: kernel(*refs[count:])


def halves(total):
    start = total // 2 // 8 * 8
    rows = -(-(total - start) // 8) * 8
    return start, (start + rows) // 2, rows, -(-rows // 16) * 16


def cost(flops, moved):
    return pl.CostEstimate(flops=int(flops), bytes_accessed=int(moved), transcendentals=0)


def params(mib=8):
    return pltpu.CompilerParams(vmem_limit_bytes=mib * 2**20)


def weigh_kernel(picks, groups, pool, table, out):
    count, stored, ngroup = picks.shape[1], pool.shape[0], table.shape[1]
    pick_hot = (lax.broadcasted_iota(jnp.int32, (stored, count), 0) == picks[...]).astype(F32)
    group_hot = (lax.broadcasted_iota(jnp.int32, (ngroup, count), 0) == groups[...]).astype(F32)
    ctf = jnp.dot(table[...], group_hot, precision=EXACT, preferred_element_type=F32).T
    chosen = lax.dot_general(pick_hot.astype(BF16), pool[...], TN, preferred_element_type=F32)
    for c in range(CYCLES):
        here = slice(c * ANG, (c + 1) * ANG)
        out[:, here] = (chosen[:, here] * ctf[:, c : c + 1]).astype(BF16)
    out[:, PIX:] = jnp.concatenate(
        [ctf * ctf, jnp.zeros((count, ANG - CYCLES), F32)], axis=1
    ).astype(BF16)


def weigh(picks, groups, pool, table):
    count = picks.shape[0]
    return pl.pallas_call(
        weigh_kernel,
        out_shape=jax.ShapeDtypeStruct((count, PIX + ANG), BF16),
        in_specs=[VMEM] * 4,
        out_specs=VMEM,
        compiler_params=params(LARGE),
        cost_estimate=cost(2 * count * 48 * PIX, 2**20),
        name="weigh",
    )(picks.reshape(1, -1), groups.reshape(1, -1), pool, table.T)


def prepare_kernel(width, place, classes, prior, halved, power, column):
    upper = place[0] == 1
    total = classes.shape[0]
    start, cut, _, _ = halves(total)
    pad = jnp.zeros((width - (total - start), ANG), F32)
    lane = lax.broadcasted_iota(jnp.int32, (width, ANG), 1)
    kept = jnp.zeros((width, ANG), F32)
    for c in range(CYCLES):
        here = slice(c * ANG, (c + 1) * ANG)
        high = jnp.concatenate([classes[start:total, here], pad], axis=0)
        mine = jnp.where(upper, high, classes[0:width, here]).astype(BF16)
        halved[:, here] = mine
        wide = mine.astype(F32)
        kept = jnp.where(lane == c, jnp.sum(wide * wide, axis=1, keepdims=True), kept)
    power[...] = kept
    turned = jnp.broadcast_to(prior[...], (ANG, ANG)).T
    high = jnp.concatenate([turned[start:total, :], pad], axis=0)
    row = lax.broadcasted_iota(jnp.int32, (width, ANG), 0)
    mine = (row >= jnp.where(upper, cut - start, 0)) & (
        row < jnp.where(upper, total - start, cut)
    )
    column[...] = jnp.where(mine, jnp.where(upper, high, turned[0:width, :]), NEGATIVE)


def prepare(width, place, classes, prior, after):
    return pl.pallas_call(
        later(functools.partial(prepare_kernel, width), len(after)),
        out_shape=(
            jax.ShapeDtypeStruct((width, PIX), BF16),
            jax.ShapeDtypeStruct((width, ANG), F32),
            jax.ShapeDtypeStruct((width, ANG), F32),
        ),
        in_specs=[ANY] * len(after) + [SMEM, VMEM, VMEM],
        out_specs=(VMEM,) * 3,
        compiler_params=params(LARGE),
        cost_estimate=cost(2 * 2**30, 2 * 2**20),
        name="prepare",
    )(*after, place, classes, prior)


def score_kernel(width, groups, span, place, shifts, halved, power, column, same, across, *refs):
    (terms, summed, stats, sides), (images, logits, *turned) = refs[:4], refs[4:]
    one = same.shape[0]
    count = images.shape[0]
    core = place[2]
    images[pl.ds(pl.multiple_of(core * one, 16), one), :] = same[...]
    images[pl.ds(pl.multiple_of((1 - core) * one, 16), one), :] = across[...]
    squares = images[:, PIX:].astype(F32)
    sides[...] = squares
    norm = lax.dot_general(power[...], squares, NT, precision=EXACT, preferred_element_type=F32)
    bias = column[:, 0:1] - 0.5 * norm

    each = ROT // groups
    top = jnp.full((width, count), NEGATIVE, F32)
    for g in range(groups):
        scores = None
        for q in range(CYCLES // span):
            block = turned[q % 2]
            for c in range(span):
                cycle = q * span + c
                image = halved[:, cycle * ANG : (cycle + 1) * ANG]
                for r in range(each):
                    block[r * width : (r + 1) * width, c * ANG : (c + 1) * ANG] = pltpu.roll(
                        image, shifts[g * each + r], 1
                    )
            part = lax.dot_general(
                block[...],
                images[:, q * span * ANG : (q + 1) * span * ANG],
                NT,
                preferred_element_type=F32,
            )
            scores = part if scores is None else scores + part
        for r in range(each):
            value = scores[r * width : (r + 1) * width, :] + bias
            logits[(g * each + r) * width : (g * each + r + 1) * width, :] = value
            top = jnp.maximum(top, value)
    top = jnp.max(top, axis=0, keepdims=True)

    def add(r, sums):
        block = pl.ds(pl.multiple_of(r * width, 16), width)
        value = jnp.exp(logits[block, :] - top)
        rounded = value.astype(BF16)
        terms[block, :] = rounded
        return sums[0] + value, sums[1] + rounded.astype(F32)

    zero = jnp.zeros((width, count), F32)
    total, rounded = lax.fori_loop(0, ROT, add, (zero, zero))
    summed[...] = rounded
    stats[0:1, :] = top
    stats[1:2, :] = jnp.sum(total, axis=0, keepdims=True)
    stats[2:, :] = jnp.zeros((6, count), F32)


def score(width, place, shifts, halved, power, column, same, across):
    groups, span = 4, 4
    one, full = same.shape
    count = 2 * one
    outs = (
        jax.ShapeDtypeStruct((ROT * width, count), BF16),
        jax.ShapeDtypeStruct((width, count), F32),
        jax.ShapeDtypeStruct((8, count), F32),
        jax.ShapeDtypeStruct((count, ANG), F32),
    )
    return pl.pallas_call(
        functools.partial(score_kernel, width, groups, span),
        out_shape=outs,
        in_specs=[SMEM, SMEM] + [VMEM] * 5,
        out_specs=(VMEM,) * 4,
        scratch_shapes=[pltpu.VMEM((count, full), BF16), pltpu.VMEM((ROT * width, count), F32)]
        + [pltpu.VMEM((ROT // groups * width, span * ANG), BF16)] * 2,
        compiler_params=params(24),
        cost_estimate=cost(10 * 2**30, 20 * 2**20),
        name="score",
    )(place, shifts, halved, power, column, same, across)


def normalize_kernel(place, own, summed, squares, *refs):
    stats, (scales, evidence, denominator, joined) = refs[:-4], refs[-4:]
    count = own.shape[1]
    for m, stat in enumerate(stats):
        joined[pl.ds(pl.multiple_of((place[1] ^ m) * 8, 8), 8), :] = stat[...]
    tops = [joined[8 * j : 8 * j + 1, :] for j in range(len(stats))]
    totals = [joined[8 * j + 1 : 8 * j + 2, :] for j in range(len(stats))]
    top = functools.reduce(jnp.maximum, tops)
    total = sum(t * jnp.exp(h - top) for h, t in zip(tops, totals))
    evidence[...] = jnp.broadcast_to(top + jnp.log(total), (8, count))
    scale = jnp.exp(own[0:1, :] - top) / total
    scales[...] = jnp.broadcast_to(scale, (ANG, count)).T
    denominator[...] = jnp.dot(
        summed[...] * scale, squares[...], precision=EXACT, preferred_element_type=F32
    )


def normalize(place, own, summed, squares, stats):
    width, count = summed.shape
    return pl.pallas_call(
        normalize_kernel,
        out_shape=(
            jax.ShapeDtypeStruct((count, ANG), F32),
            jax.ShapeDtypeStruct((8, count), F32),
            jax.ShapeDtypeStruct((width, ANG), F32),
        ),
        in_specs=[SMEM] + [VMEM] * (3 + len(stats)),
        out_specs=(VMEM,) * 3,
        scratch_shapes=[pltpu.VMEM((8 * len(stats), count), F32)],
        compiler_params=params(),
        cost_estimate=cost(2**30, 2**20),
        name="normalize",
    )(place, own, summed, squares, *stats)


def merge_kernel(place, own, other, out):
    lower = place[2] == 0
    first, second = (jnp.where(lower, a[...], b[...]) for a, b in ((own, other), (other, own)))
    top = jnp.maximum(first[0:1], second[0:1])
    out[...] = jnp.zeros_like(out)
    out[0:1, :] = top
    out[1:2, :] = first[1:2] * jnp.exp(first[0:1] - top) + second[1:2] * jnp.exp(second[0:1] - top)


def merge(place, own, other):
    return pl.pallas_call(
        merge_kernel,
        out_shape=jax.ShapeDtypeStruct(own.shape, F32),
        in_specs=[SMEM, VMEM, VMEM],
        out_specs=VMEM,
        compiler_params=params(4),
        cost_estimate=cost(0, 0),
        name="merge",
    )(place, own, other)


def update_kernel(width, rows, span, place, shifts, terms, same, across, scales, *refs):
    below, (out, product) = refs[:-2], refs[-2:]
    for b in below:
        high = b[...].astype(BF16).astype(F32)
        both = high + pltpu.roll(b[...] - high, CYCLES, 1)
        out[:, span * ANG :] = both[:rows].astype(BF16)
    lower = place[2] == 0
    images = [jnp.where(lower, a[...], b[...]) for a, b in ((same, across), (across, same))]
    images = jnp.concatenate(images, axis=0).astype(F32)
    scaled = (images * scales[:, 0:1]).astype(BF16)
    product[...] = jnp.dot(terms[...], scaled, preferred_element_type=F32).astype(BF16)
    for j in range(span):
        here = slice(j * ANG, (j + 1) * ANG)
        total = jnp.zeros((width, ANG), F32)
        for r in range(ROT):
            back = (ANG - shifts[r]) & (ANG - 1)
            turned = pltpu.roll(product[r * width : (r + 1) * width, here], back, 1)
            total = total + turned.astype(F32)
        out[:, here] = total[:rows].astype(BF16)


def update(width, rows, first, cycles, place, shifts, terms, same, across, scales, below, after):
    one = same.shape[0]
    block = pl.BlockSpec((one, cycles * ANG), lambda i: (0, base))
    base = first // cycles
    whole = lambda a: pl.BlockSpec(a.shape, lambda i: (0, 0))
    out = jax.ShapeDtypeStruct((rows, (cycles + len(below)) * ANG), BF16)
    return pl.pallas_call(
        later(functools.partial(update_kernel, width, rows, cycles), len(after)),
        grid=(1,),
        out_shape=out,
        in_specs=[ANY] * len(after)
        + [
            SMEM,
            SMEM,
            whole(terms),
            block,
            block,
            whole(scales),
        ]
        + [whole(b) for b in below],
        out_specs=whole(out),
        scratch_shapes=[pltpu.VMEM((ROT * width, cycles * ANG), BF16)],
        compiler_params=params(20),
        cost_estimate=cost(3 * 2**30, 4 * 2**20),
        name="update",
    )(*after, place, shifts, terms, same, across, scales, *below)


def divide_kernel(first, one, two, *refs):
    share, out = refs[0], refs[-1]
    rows, span = out.shape
    lane = lax.broadcasted_iota(jnp.int32, (rows, ANG), 1)
    if len(refs) == 2 and first == 0:
        below = one[:, span:].astype(F32) + two[:, span:].astype(F32)
        below = below + pltpu.roll(below, ANG - CYCLES, 1)
        share[...] = 1.0 / (below + PRIOR_WEIGHT)
    for j in range(span // ANG):
        here = slice(j * ANG, (j + 1) * ANG)
        total = one[:, here].astype(F32) + two[:, here].astype(F32)
        cycle = jnp.where(lane == first + j, share[...], 0.0)
        out[:, here] = (total * jnp.sum(cycle, axis=1, keepdims=True)).astype(BF16)


def divide(first, cycles, one, two, share, after):
    rows = one.shape[0]
    outs = () if share else (jax.ShapeDtypeStruct((rows, ANG), F32),)
    outs += (jax.ShapeDtypeStruct((rows, cycles * ANG), BF16),)
    return pl.pallas_call(
        later(functools.partial(divide_kernel, first), len(after)),
        out_shape=outs,
        in_specs=[ANY] * len(after) + [VMEM] * (2 + len(share)),
        out_specs=(VMEM,) * len(outs),
        compiler_params=params(8),
        cost_estimate=cost(2**28, 0),
        name="divide",
    )(*after, one, two, *share)


def blend_kernel(chunks, place, classes, *refs):
    out = refs[-1]
    total = classes.shape[0]
    start, cut, rows, _ = halves(total)
    upper = place[0] == 1
    at = 0
    for p in range(chunks):
        mine, other = refs[2 * p : 2 * p + 2]
        span = mine.shape[1]
        here = slice(at, at + span)
        at += span
        first, second = mine[...].astype(F32), other[...].astype(F32)
        low = jnp.where(upper, second, first)
        high = jnp.where(upper, first, second)
        low = jnp.concatenate([low, jnp.zeros((total - rows, span), F32)], axis=0)
        high = jnp.concatenate([jnp.zeros((start, span), F32), high[: total - start]], axis=0)
        row = lax.broadcasted_iota(jnp.int32, (total, span), 0)
        step = jnp.where(row < cut, low, high)
        out[:, here] = (1.0 - STEP_WEIGHT) * classes[:, here] + STEP_WEIGHT * step


def blend(first, place, classes, updates, before):
    span = sum(mine.shape[1] for mine, _ in updates)
    block = pl.BlockSpec((classes.shape[0], span), lambda i: (0, first * ANG // span))
    flat = [u for pair in updates for u in pair]
    return pl.pallas_call(
        functools.partial(blend_kernel, len(updates)),
        grid=(1,),
        out_shape=jax.ShapeDtypeStruct(classes.shape, F32),
        in_specs=[SMEM, block]
        + [pl.BlockSpec(u.shape, lambda i: (0, 0)) for u in flat]
        + [ANY] * len(before),
        out_specs=block,
        input_output_aliases={2 + len(flat): 0} if before else {},
        compiler_params=params(),
        cost_estimate=cost(2**30, 2**20),
        name="blend",
    )(place, classes, *flat, *before)


def halved(pool, picks, groups, ctf_table, shifts, classes, log_prior):
    total = classes.shape[0]
    _, _, rows, width = halves(total)
    axes = ("particle", "cls")
    z, cls = lax.axis_index("particle"), lax.axis_index("cls")
    chip, core = cls // 2, cls % 2
    half = z % 2
    place = jnp.stack([half, half * 2 + chip, core]).astype(jnp.int32)
    prior = jnp.pad(log_prior, (0, ANG - total)).reshape(1, ANG)

    def swap(a, mask):
        return lax.ppermute(a, axes, [(i, i ^ mask) for i in range(16)])

    CORE, CHIP, NEXT, SAME = 1, 2, 4, 8

    own = weigh(picks, groups, pool, ctf_table)
    beside = swap(own, NEXT)
    own_x = swap(own, CHIP)
    beside_x = swap(own, NEXT + CHIP)
    halved, power, column = prepare(width, place, classes, prior, (own,))
    own_x, beside, beside_x, halved = lax.optimization_barrier((own_x, beside, beside_x, halved))
    pairs = [
        (jnp.where(chip == 1, x, a), jnp.where(chip == 1, a, x))
        for a, x in ((own, own_x), (beside, beside_x))
    ]
    odd = z % 2 == 1
    low = [jnp.where(odd, b, a) for a, b in zip(*pairs)]
    high = [jnp.where(odd, a, b) for a, b in zip(*pairs)]
    same = jnp.concatenate(low + high, axis=0)
    across = swap(same, CORE)

    terms, summed, own_stat, squares = score(
        width, place, shifts, halved, power, column, same, across
    )

    stat = merge(place, own_stat, swap(own_stat, CORE))
    stats = [stat] + [swap(stat, m) for m in (CHIP, NEXT, NEXT + CHIP)]
    scales, evidence, below = normalize(place, own_stat, summed, squares, stats)

    mine, other, ratios, others, share = [], [], [], [], []
    last = len(CHUNKS) - 1
    firsts = [sum(CHUNKS[:p]) for p in range(len(CHUNKS))]

    def finish(p):
        after = tuple(ratios[-1:])
        *new, ratio = divide(firsts[p], CHUNKS[p], mine[p], other[p], tuple(share), after)
        share.extend(new)
        ratios.append(ratio)
        others.append(swap(ratios[p], NEXT))

    for p, cycles in enumerate(CHUNKS):
        after, extra = tuple(mine[-1:]), () if p else (below,)
        part = update(
            width, rows, firsts[p], cycles, place, shifts, terms, same, across, scales, extra, after
        )
        mine.append(part)
        other.append(swap(part, SAME))
    for p in range(last + 1):
        finish(p)
    both = list(zip(ratios, others))
    updated = blend(0, place, classes, both[:last], ())
    updated = blend(firsts[last], place, classes, both[last:], (updated,))
    count = picks.shape[0]
    by_shard = evidence[0].reshape(2, 2, 2, count)
    log_evidence = jnp.take(by_shard, z % 2, axis=1)
    return (updated, jnp.transpose(log_evidence, (1, 0, 2)).reshape(4 * count))


def joined(part, axis, combine):
    gathered = jax.tree.map(lambda a: lax.all_gather(a, axis), part)

    def take(source):
        return jax.tree.map(lambda a: lax.dynamic_index_in_dim(a, source, 0, False), gathered)

    return lax.fori_loop(
        1, lax.axis_size(axis), lambda source, state: combine(state, take(source)), take(0)
    )


def angle_major(images):
    count_rows = images.shape[0]
    return jnp.transpose(images.reshape(count_rows, CYCLES, ANG), (2, 1, 0)).reshape(
        ANG * CYCLES, count_rows
    )


def turned_view(doubled, offset):
    return lax.dynamic_slice_in_dim(doubled, offset * CYCLES, ANG * CYCLES, 0)


def all_scores(doubled, refs_major, shift_blocks):
    block_len = shift_blocks.shape[1]

    def single(shift_row):
        outputs = []
        for slot in range(block_len):
            piece = turned_view(doubled, shift_row[slot])
            outputs.append(
                lax.dot_general(
                    piece, refs_major, (((0,), (0,)), ((), ())), preferred_element_type=jnp.float32
                )
            )
        return jnp.stack(outputs, axis=0)

    partial_value = lax.map(single, shift_blocks)
    return partial_value.reshape(-1, partial_value.shape[2], partial_value.shape[3])


def class_numerator(doubled, weights, shift_blocks):
    nblocks, block_len = shift_blocks.shape
    weight_blocks = weights.reshape(nblocks, block_len, weights.shape[1], weights.shape[2])

    def advance(carried, pieces):
        shift_row, weight_block = pieces
        for slot in range(block_len):
            piece = turned_view(doubled, shift_row[slot])
            carried = carried + jnp.dot(
                piece, weight_block[slot], preferred_element_type=jnp.float32
            )
        return (carried, None)

    start_value = jnp.zeros((ANG * CYCLES, weights.shape[2]), jnp.float32)
    numerator_major, _ = lax.scan(advance, start_value, (shift_blocks, weight_blocks))
    classes_here = weights.shape[2]
    return jnp.transpose(numerator_major.reshape(ANG, CYCLES, classes_here), (2, 1, 0)).reshape(
        classes_here, CYCLES * ANG
    )


def merge_softmax(earlier, later):
    row_top = jnp.maximum(earlier[0], later[0])
    row_total = earlier[1] * jnp.exp(earlier[0] - row_top) + later[1] * jnp.exp(later[0] - row_top)
    return (row_top, row_total)


def whole_sum(pool, picks, groups, ctf_table, shifts, classes, log_prior):
    chosen = jnp.take(pool, picks, axis=0)
    count_local = chosen.shape[0]
    onehot_rows = (
        groups[:, None] == jnp.arange(ctf_table.shape[0], dtype=jnp.int32)[None, :]
    ).astype(jnp.float32)
    ctf_rows = jnp.dot(onehot_rows, ctf_table, precision=lax.Precision.HIGHEST)
    weighted = (
        (chosen.astype(jnp.float32).reshape(count_local, CYCLES, ANG) * ctf_rows[:, :, None])
        .reshape(count_local, CYCLES * ANG)
        .astype(jnp.bfloat16)
    )
    ctf_sq = (ctf_rows * ctf_rows).astype(jnp.bfloat16)
    batch_rows, batch_sq = (
        lax.all_gather(weighted, "cls", axis=0, tiled=True),
        lax.all_gather(ctf_sq, "cls", axis=0, tiled=True),
    )
    batch_major = angle_major(batch_rows)
    doubled = jnp.concatenate([batch_major, batch_major], axis=0)
    refs = classes.astype(jnp.bfloat16)
    refs_major = angle_major(refs)
    cycle_power = jnp.sum(
        jnp.square(refs.astype(jnp.float32)).reshape(classes.shape[0], CYCLES, ANG), axis=2
    )
    block_len = math.gcd(ROT, 6)
    shift_blocks = shifts.reshape(ROT // block_len, block_len)
    scores = all_scores(doubled, refs_major, shift_blocks)
    norm_term = jnp.dot(
        batch_sq.astype(jnp.float32), cycle_power.T, precision=lax.Precision.HIGHEST
    )
    logits = scores - 0.5 * norm_term[None, :, :] + log_prior[None, None, :]
    local_top = jnp.max(logits, axis=(0, 2))
    local_total = jnp.sum(jnp.exp(logits - local_top[None, :, None]), axis=(0, 2))
    row_top, row_total = joined((local_top, local_total), "cls", merge_softmax)
    exp_terms = jnp.exp(logits - row_top[None, :, None])
    weights = (exp_terms / row_total[None, :, None]).astype(jnp.bfloat16)
    log_evidence = row_top + jnp.log(row_total)
    numerator = class_numerator(doubled, weights, shift_blocks)
    weight_sum = jnp.sum(weights.astype(jnp.float32), axis=0)
    denominator = lax.dot_general(
        weight_sum,
        batch_sq.astype(jnp.float32),
        (((0,), (0,)), ((), ())),
        precision=lax.Precision.HIGHEST,
    )
    numerator, denominator = lax.psum((numerator, denominator), "particle")
    spread = jnp.repeat(denominator, ANG, axis=1)
    updated = (1.0 - STEP_WEIGHT) * classes + STEP_WEIGHT * numerator / (spread + PRIOR_WEIGHT)
    return (updated, log_evidence)


def solution(mesh):
    in_specs = (
        P(("groups", "particle", "cls"), None),
        P(("groups", "particle", "cls")),
        P(("groups", "particle", "cls")),
        P("groups", None),
        P("groups"),
        P(("groups", "cls"), None),
        P(("groups", "cls")),
    )
    out_specs = (P(("groups", "cls"), None), P(("groups", "particle")))
    quad = mesh.shape["particle"] == 4 and mesh.shape["cls"] == 4
    return jax.shard_map(
        halved if quad else whole_sum, mesh=mesh, in_specs=in_specs, out_specs=out_specs, check_vma=False
    )
```

```python
import functools
import math

import jax
import jax.numpy as jnp
from jax import lax
from jax.experimental import pallas as pl
from jax.experimental.pallas import tpu as pltpu
from jax.sharding import PartitionSpec as P

CYCLES = 32
ANG = 128
ROT = 36
PIX = CYCLES * ANG

STEP_WEIGHT = 0.5
PRIOR_WEIGHT = 1.0

VMEM = pl.BlockSpec(memory_space=pltpu.VMEM)
ANY = pl.BlockSpec(memory_space=pl.ANY)
SMEM = pl.BlockSpec(memory_space=pltpu.SMEM)
F32 = jnp.float32
BF16 = jnp.bfloat16
NT = (((1,), (1,)), ((), ()))
TN = (((0,), (0,)), ((), ()))
EXACT = lax.Precision.HIGHEST
NEGATIVE = -1e30
CHUNKS = (8, 8, 8, 8)
LARGE = 58
QUARTERS = 4


def later(kernel, count):
    return lambda *refs: kernel(*refs[count:])


def halves(total):
    half = total // 2
    full = half // 8 * 8
    return half, full, half - full, -(-half // 16) * 16


def cost(flops, moved):
    return pl.CostEstimate(flops=int(flops), bytes_accessed=int(moved), transcendentals=0)


def params(mib=8):
    return pltpu.CompilerParams(vmem_limit_bytes=mib * 2**20)


def weigh_kernel(picks, groups, pool, table, out):
    count, stored, ngroup = picks.shape[1], pool.shape[0], table.shape[1]
    pick_hot = (lax.broadcasted_iota(jnp.int32, (stored, count), 0) == picks[...]).astype(F32)
    group_hot = (lax.broadcasted_iota(jnp.int32, (ngroup, count), 0) == groups[...]).astype(F32)
    ctf = jnp.dot(table[...], group_hot, precision=EXACT, preferred_element_type=F32).T
    chosen = lax.dot_general(pick_hot.astype(BF16), pool[...], TN, preferred_element_type=F32)
    for c in range(CYCLES):
        here = slice(c * ANG, (c + 1) * ANG)
        out[:, here] = (chosen[:, here] * ctf[:, c : c + 1]).astype(BF16)
    out[:, PIX:] = jnp.concatenate(
        [ctf * ctf, jnp.zeros((count, ANG - CYCLES), F32)], axis=1
    ).astype(BF16)


def weigh(picks, groups, pool, table):
    count = picks.shape[0]
    return pl.pallas_call(
        weigh_kernel,
        out_shape=jax.ShapeDtypeStruct((count, PIX + ANG), BF16),
        in_specs=[VMEM] * 4,
        out_specs=VMEM,
        compiler_params=params(LARGE),
        cost_estimate=cost(2 * count * 48 * PIX, 2**20),
        name="weigh",
    )(picks.reshape(1, -1), groups.reshape(1, -1), pool, table.T)


def prepare_kernel(width, place, classes, prior, halved, power, column):
    upper = place[0] == 1
    total = classes.shape[0]
    half, full, rest, _ = halves(total)
    pad = jnp.zeros((width - (total - full), ANG), F32)
    lane = lax.broadcasted_iota(jnp.int32, (width, ANG), 1)

    def mine(low, high):
        high = pltpu.roll(jnp.concatenate([high, pad], axis=0), width - rest, 0)
        return jnp.where(upper, high, low)

    kept = jnp.zeros((width, ANG), F32)
    for c in range(CYCLES):
        here = slice(c * ANG, (c + 1) * ANG)
        part = mine(classes[0:width, here], classes[full:total, here]).astype(BF16)
        halved[:, here] = part
        wide = part.astype(F32)
        kept = jnp.where(lane == c, jnp.sum(wide * wide, axis=1, keepdims=True), kept)
    power[...] = kept
    turned = jnp.broadcast_to(prior[...], (ANG, ANG)).T
    row = lax.broadcasted_iota(jnp.int32, (width, ANG), 0)
    column[...] = jnp.where(row < half, mine(turned[0:width], turned[full:total]), NEGATIVE)


def prepare(width, place, classes, prior, after):
    return pl.pallas_call(
        later(functools.partial(prepare_kernel, width), len(after)),
        out_shape=(
            jax.ShapeDtypeStruct((width, PIX), BF16),
            jax.ShapeDtypeStruct((width, ANG), F32),
            jax.ShapeDtypeStruct((width, ANG), F32),
        ),
        in_specs=[ANY] * len(after) + [SMEM, VMEM, VMEM],
        out_specs=(VMEM,) * 3,
        compiler_params=params(LARGE),
        cost_estimate=cost(2 * 2**30, 2 * 2**20),
        name="prepare",
    )(*after, place, classes, prior)


def score_kernel(width, groups, span, place, shifts, halved, power, column, same, across, *refs):
    (terms, summed, stats, sides), (images, logits, *turned) = refs[:4], refs[4:]
    one = same.shape[0]
    count = images.shape[0]
    core = place[2]
    images[pl.ds(pl.multiple_of(core * one, 16), one), :] = same[...]
    images[pl.ds(pl.multiple_of((1 - core) * one, 16), one), :] = across[...]
    squares = images[:, PIX:].astype(F32)
    sides[...] = squares
    norm = lax.dot_general(power[...], squares, NT, precision=EXACT, preferred_element_type=F32)
    bias = column[:, 0:1] - 0.5 * norm

    each = ROT // groups
    top = jnp.full((width, count), NEGATIVE, F32)
    for g in range(groups):
        scores = None
        for q in range(CYCLES // span):
            block = turned[q % 2]
            for c in range(span):
                cycle = q * span + c
                image = halved[:, cycle * ANG : (cycle + 1) * ANG]
                for r in range(each):
                    block[r * width : (r + 1) * width, c * ANG : (c + 1) * ANG] = pltpu.roll(
                        image, shifts[g * each + r], 1
                    )
            part = lax.dot_general(
                block[...],
                images[:, q * span * ANG : (q + 1) * span * ANG],
                NT,
                preferred_element_type=F32,
            )
            scores = part if scores is None else scores + part
        for r in range(each):
            value = scores[r * width : (r + 1) * width, :] + bias
            logits[(g * each + r) * width : (g * each + r + 1) * width, :] = value
            top = jnp.maximum(top, value)
    top = jnp.max(top, axis=0, keepdims=True)

    def add(r, sums):
        block = pl.ds(pl.multiple_of(r * width, 16), width)
        value = jnp.exp(logits[block, :] - top)
        rounded = value.astype(BF16)
        terms[block, :] = rounded
        return sums[0] + value, sums[1] + rounded.astype(F32)

    zero = jnp.zeros((width, count), F32)
    total, rounded = lax.fori_loop(0, ROT, add, (zero, zero))
    summed[...] = rounded
    stats[0:1, :] = top
    stats[1:2, :] = jnp.sum(total, axis=0, keepdims=True)
    stats[2:, :] = jnp.zeros((6, count), F32)


def score(width, place, shifts, halved, power, column, same, across):
    groups, span = 4, 4
    one, full = same.shape
    count = 2 * one
    outs = (
        jax.ShapeDtypeStruct((ROT * width, count), BF16),
        jax.ShapeDtypeStruct((width, count), F32),
        jax.ShapeDtypeStruct((8, count), F32),
        jax.ShapeDtypeStruct((count, ANG), F32),
    )
    return pl.pallas_call(
        functools.partial(score_kernel, width, groups, span),
        out_shape=outs,
        in_specs=[SMEM, SMEM] + [VMEM] * 5,
        out_specs=(VMEM,) * 4,
        scratch_shapes=[pltpu.VMEM((count, full), BF16), pltpu.VMEM((ROT * width, count), F32)]
        + [pltpu.VMEM((ROT // groups * width, span * ANG), BF16)] * 2,
        compiler_params=params(24),
        cost_estimate=cost(10 * 2**30, 20 * 2**20),
        name="score",
    )(place, shifts, halved, power, column, same, across)


def normalize_kernel(place, own, summed, squares, *refs):
    stats, (scales, evidence, denominator, joined) = refs[:-4], refs[-4:]
    count = own.shape[1]
    for m, stat in enumerate(stats):
        joined[pl.ds(pl.multiple_of((place[1] ^ m) * 8, 8), 8), :] = stat[...]
    tops = [joined[8 * j : 8 * j + 1, :] for j in range(len(stats))]
    totals = [joined[8 * j + 1 : 8 * j + 2, :] for j in range(len(stats))]
    top = functools.reduce(jnp.maximum, tops)
    total = sum(t * jnp.exp(h - top) for h, t in zip(tops, totals))
    evidence[...] = jnp.broadcast_to(top + jnp.log(total), (8, count))
    scale = jnp.exp(own[0:1, :] - top) / total
    scales[...] = jnp.broadcast_to(scale, (ANG, count)).T
    denominator[...] = jnp.dot(
        summed[...] * scale, squares[...], precision=EXACT, preferred_element_type=F32
    )


def normalize(place, own, summed, squares, stats):
    width, count = summed.shape
    return pl.pallas_call(
        normalize_kernel,
        out_shape=(
            jax.ShapeDtypeStruct((count, ANG), F32),
            jax.ShapeDtypeStruct((8, count), F32),
            jax.ShapeDtypeStruct((width, ANG), F32),
        ),
        in_specs=[SMEM] + [VMEM] * (3 + len(stats)),
        out_specs=(VMEM,) * 3,
        scratch_shapes=[pltpu.VMEM((8 * len(stats), count), F32)],
        compiler_params=params(),
        cost_estimate=cost(2**30, 2**20),
        name="normalize",
    )(place, own, summed, squares, *stats)


def merge_kernel(place, own, other, out):
    lower = place[2] == 0
    first, second = (jnp.where(lower, a[...], b[...]) for a, b in ((own, other), (other, own)))
    top = jnp.maximum(first[0:1], second[0:1])
    out[...] = jnp.zeros_like(out)
    out[0:1, :] = top
    out[1:2, :] = first[1:2] * jnp.exp(first[0:1] - top) + second[1:2] * jnp.exp(second[0:1] - top)


def merge(place, own, other):
    return pl.pallas_call(
        merge_kernel,
        out_shape=jax.ShapeDtypeStruct(own.shape, F32),
        in_specs=[SMEM, VMEM, VMEM],
        out_specs=VMEM,
        compiler_params=params(4),
        cost_estimate=cost(0, 0),
        name="merge",
    )(place, own, other)


def update_kernel(total, first, span, place, shifts, terms, same, across, scales, *refs):
    below, (out, product) = refs[:-2], refs[-2:]
    _, full, rest, width = halves(total)
    wide = span // QUARTERS
    sent = QUARTERS * full + 8
    lower = place[2] == 0
    part = slice(first * ANG, (first + span) * ANG)
    images = [jnp.where(lower, a[:, part], b[:, part]) for a, b in ((same, across), (across, same))]
    images = jnp.concatenate(images, axis=0).astype(F32)
    scaled = (images * scales[:, 0:1]).astype(BF16)
    product[...] = jnp.dot(terms[...], scaled, preferred_element_type=F32).astype(BF16)
    row = lax.broadcasted_iota(jnp.int32, (8, ANG), 0)
    for i in range(wide):
        there = slice(i * ANG, (i + 1) * ANG)
        tail = jnp.zeros((8, ANG), F32)
        for q in range(QUARTERS):
            j = q * wide + i
            sums = jnp.zeros((width, ANG), F32)
            for r in range(ROT):
                back = (ANG - shifts[r]) & (ANG - 1)
                turned = pltpu.roll(
                    product[r * width : (r + 1) * width, j * ANG : (j + 1) * ANG], back, 1
                )
                sums = sums + turned.astype(F32)
            out[q * full : (q + 1) * full, there] = sums[:full].astype(BF16)
            moved = pltpu.roll(sums[full : full + 8], q * rest, 0) if q else sums[full : full + 8]
            tail = jnp.where((row >= q * rest) & (row < (q + 1) * rest), moved, tail)
        out[sent - 8 : sent, there] = tail.astype(BF16)
    for b in below:
        value = b[0 : full + 8, :]
        high = value.astype(BF16).astype(F32)
        both = high + pltpu.roll(value - high, CYCLES, 1)
        out[sent : sent + 32, 0:ANG] = both[0:32].astype(BF16)
        out[sent : sent + 32, ANG : 2 * ANG] = both[full - 24 : full + 8].astype(BF16)


def update(total, first, cycles, place, shifts, terms, same, across, scales, below, after):
    _, full, _, width = halves(total)
    rows = QUARTERS * full + 8 + 32 * len(below)
    return pl.pallas_call(
        later(functools.partial(update_kernel, total, first, cycles), len(after)),
        out_shape=jax.ShapeDtypeStruct((rows, cycles // QUARTERS * ANG), BF16),
        in_specs=[ANY] * len(after) + [SMEM, SMEM] + [VMEM] * (4 + len(below)),
        out_specs=VMEM,
        scratch_shapes=[pltpu.VMEM((ROT * width, cycles * ANG), BF16)],
        compiler_params=params(20),
        cost_estimate=cost(3 * 2**30, 4 * 2**20),
        name="update",
    )(*after, place, shifts, terms, same, across, scales, *below)


def divide_kernel(total, first, one, two, *refs):
    share, out = refs[0], refs[-1]
    _, full, rest, _ = halves(total)
    sent, wide = out.shape[0], out.shape[1] // ANG
    lane = lax.broadcasted_iota(jnp.int32, (full + 8, ANG), 1)
    row = lax.broadcasted_iota(jnp.int32, (8, ANG), 0)
    if first == 0:
        below = one[sent:, :].astype(F32) + two[sent:, :].astype(F32)
        below = jnp.concatenate([below[0:24, 0:ANG], below[32 - (full - 16) :, ANG:]], axis=0)
        below = below + pltpu.roll(below, ANG - CYCLES, 1)
        share[...] = 1.0 / (below + PRIOR_WEIGHT)
    for i in range(wide):
        there = slice(i * ANG, (i + 1) * ANG)
        tail = jnp.zeros((8, ANG), F32)
        for q in range(QUARTERS):
            cycle = jnp.where(lane == first + q * wide + i, share[...], 0.0)
            factor = jnp.broadcast_to(jnp.sum(cycle, axis=1, keepdims=True), (full + 8, ANG))
            here = slice(q * full, (q + 1) * full)
            sums = one[here, there].astype(F32) + two[here, there].astype(F32)
            out[here, there] = (sums * factor[:full]).astype(BF16)
            moved = pltpu.roll(factor[full:], q * rest, 0) if q else factor[full:]
            tail = jnp.where((row >= q * rest) & (row < (q + 1) * rest), moved, tail)
        sums = one[sent - 8 : sent, there].astype(F32) + two[sent - 8 : sent, there].astype(F32)
        out[sent - 8 : sent, there] = (sums * tail).astype(BF16)


def divide(total, first, cycles, one, two, share, after):
    _, full, _, _ = halves(total)
    outs = () if share else (jax.ShapeDtypeStruct((full + 8, ANG), F32),)
    outs += (jax.ShapeDtypeStruct((QUARTERS * full + 8, cycles // QUARTERS * ANG), BF16),)
    return pl.pallas_call(
        later(functools.partial(divide_kernel, total, first), len(after)),
        out_shape=outs,
        in_specs=[ANY] * len(after) + [VMEM] * (2 + len(share)),
        out_specs=(VMEM,) * len(outs),
        compiler_params=params(8),
        cost_estimate=cost(2**28, 0),
        name="divide",
    )(*after, one, two, *share)


def blend_kernel(chunks, place, classes, *refs):
    out = refs[-1]
    total = classes.shape[0]
    half, full, rest, _ = halves(total)
    upper = place[0] == 1
    span = refs[0].shape[1]
    row = lax.broadcasted_iota(jnp.int32, (full + 16, span), 0)
    none = jnp.zeros((8, span), F32)
    for p in range(chunks):
        mine, other = refs[2 * p : 2 * p + 2]
        ends = [a[QUARTERS * full :, :].astype(F32) for a in (mine, other)]
        for q in range(QUARTERS):
            rows = []
            for a, end in zip((mine, other), ends):
                end = pltpu.roll(end, 8 - q * rest, 0) if q else end
                rows.append((a[q * full : (q + 1) * full, :].astype(F32), end))
            low, low_end = (jnp.where(upper, b, a) for a, b in zip(*rows))
            high, high_end = (jnp.where(upper, a, b) for a, b in zip(*rows))
            high = pltpu.roll(jnp.concatenate([high, high_end, none], axis=0), rest, 0)
            low_end = jnp.concatenate([low_end, jnp.zeros((full + 8, span), F32)], axis=0)
            upper_rows = jnp.where(row < rest, low_end, high)
            step = jnp.concatenate([low, upper_rows[: total - full]], axis=0)
            at = slice((p * QUARTERS + q) * span, (p * QUARTERS + q + 1) * span)
            out[:, at] = (1.0 - STEP_WEIGHT) * classes[:, at] + STEP_WEIGHT * step


def blend(first, place, classes, updates, before):
    span = QUARTERS * sum(mine.shape[1] for mine, _ in updates)
    block = pl.BlockSpec((classes.shape[0], span), lambda i: (0, first * ANG // span))
    flat = [u for pair in updates for u in pair]
    return pl.pallas_call(
        functools.partial(blend_kernel, len(updates)),
        grid=(1,),
        out_shape=jax.ShapeDtypeStruct(classes.shape, F32),
        in_specs=[SMEM, block]
        + [pl.BlockSpec(u.shape, lambda i: (0, 0)) for u in flat]
        + [ANY] * len(before),
        out_specs=block,
        input_output_aliases={2 + len(flat): 0} if before else {},
        compiler_params=params(),
        cost_estimate=cost(2**30, 2**20),
        name="blend",
    )(place, classes, *flat, *before)


def halved(pool, picks, groups, ctf_table, shifts, classes, log_prior):
    total = classes.shape[0]
    width = halves(total)[-1]
    axes = ("particle", "cls")
    z, cls = lax.axis_index("particle"), lax.axis_index("cls")
    chip, core = cls // 2, cls % 2
    half = z % 2
    place = jnp.stack([half, half * 2 + chip, core]).astype(jnp.int32)
    prior = jnp.pad(log_prior, (0, ANG - total)).reshape(1, ANG)

    def swap(a, mask):
        return lax.ppermute(a, axes, [(i, i ^ mask) for i in range(16)])

    CORE, CHIP, NEXT, SAME = 1, 2, 4, 8

    own = weigh(picks, groups, pool, ctf_table)
    beside = swap(own, NEXT)
    own_x = swap(own, CHIP)
    beside_x = swap(own, NEXT + CHIP)
    halved, power, column = prepare(width, place, classes, prior, (own,))
    own_x, beside, beside_x, halved = lax.optimization_barrier((own_x, beside, beside_x, halved))
    pairs = [
        (jnp.where(chip == 1, x, a), jnp.where(chip == 1, a, x))
        for a, x in ((own, own_x), (beside, beside_x))
    ]
    odd = z % 2 == 1
    low = [jnp.where(odd, b, a) for a, b in zip(*pairs)]
    high = [jnp.where(odd, a, b) for a, b in zip(*pairs)]
    same = jnp.concatenate(low + high, axis=0)
    across = swap(same, CORE)

    terms, summed, own_stat, squares = score(
        width, place, shifts, halved, power, column, same, across
    )

    stat = merge(place, own_stat, swap(own_stat, CORE))
    stats = [stat] + [swap(stat, m) for m in (CHIP, NEXT, NEXT + CHIP)]
    scales, evidence, below = normalize(place, own_stat, summed, squares, stats)

    mine, other, ratios, others, share = [], [], [], [], []
    last = len(CHUNKS) - 1
    firsts = [sum(CHUNKS[:p]) for p in range(len(CHUNKS))]

    def finish(p):
        after = tuple(ratios[-1:])
        *new, ratio = divide(total, firsts[p], CHUNKS[p], mine[p], other[p], tuple(share), after)
        share.extend(new)
        ratios.append(ratio)
        others.append(swap(ratios[p], NEXT))

    for p, cycles in enumerate(CHUNKS):
        after, extra = tuple(mine[-1:]), () if p else (below,)
        part = update(
            total, firsts[p], cycles, place, shifts, terms, same, across, scales, extra, after
        )
        mine.append(part)
        other.append(swap(part, SAME))
    for p in range(last + 1):
        finish(p)
    both = list(zip(ratios, others))
    cut = 2
    updated = blend(0, place, classes, both[:cut], ())
    updated = blend(firsts[cut], place, classes, both[cut:], (updated,))
    count = picks.shape[0]
    by_shard = evidence[0].reshape(2, 2, 2, count)
    log_evidence = jnp.take(by_shard, z % 2, axis=1)
    return (updated, jnp.transpose(log_evidence, (1, 0, 2)).reshape(4 * count))


def joined(part, axis, combine):
    gathered = jax.tree.map(lambda a: lax.all_gather(a, axis), part)

    def take(source):
        return jax.tree.map(lambda a: lax.dynamic_index_in_dim(a, source, 0, False), gathered)

    return lax.fori_loop(
        1, lax.axis_size(axis), lambda source, state: combine(state, take(source)), take(0)
    )


def angle_major(images):
    count_rows = images.shape[0]
    return jnp.transpose(images.reshape(count_rows, CYCLES, ANG), (2, 1, 0)).reshape(
        ANG * CYCLES, count_rows
    )


def turned_view(doubled, offset):
    return lax.dynamic_slice_in_dim(doubled, offset * CYCLES, ANG * CYCLES, 0)


def all_scores(doubled, refs_major, shift_blocks):
    block_len = shift_blocks.shape[1]

    def single(shift_row):
        outputs = []
        for slot in range(block_len):
            piece = turned_view(doubled, shift_row[slot])
            outputs.append(
                lax.dot_general(
                    piece, refs_major, (((0,), (0,)), ((), ())), preferred_element_type=jnp.float32
                )
            )
        return jnp.stack(outputs, axis=0)

    partial_value = lax.map(single, shift_blocks)
    return partial_value.reshape(-1, partial_value.shape[2], partial_value.shape[3])


def class_numerator(doubled, weights, shift_blocks):
    nblocks, block_len = shift_blocks.shape
    weight_blocks = weights.reshape(nblocks, block_len, weights.shape[1], weights.shape[2])

    def advance(carried, pieces):
        shift_row, weight_block = pieces
        for slot in range(block_len):
            piece = turned_view(doubled, shift_row[slot])
            carried = carried + jnp.dot(
                piece, weight_block[slot], preferred_element_type=jnp.float32
            )
        return (carried, None)

    start_value = jnp.zeros((ANG * CYCLES, weights.shape[2]), jnp.float32)
    numerator_major, _ = lax.scan(advance, start_value, (shift_blocks, weight_blocks))
    classes_here = weights.shape[2]
    return jnp.transpose(numerator_major.reshape(ANG, CYCLES, classes_here), (2, 1, 0)).reshape(
        classes_here, CYCLES * ANG
    )


def merge_softmax(earlier, later):
    row_top = jnp.maximum(earlier[0], later[0])
    row_total = earlier[1] * jnp.exp(earlier[0] - row_top) + later[1] * jnp.exp(later[0] - row_top)
    return (row_top, row_total)


def whole_sum(pool, picks, groups, ctf_table, shifts, classes, log_prior):
    chosen = jnp.take(pool, picks, axis=0)
    count_local = chosen.shape[0]
    onehot_rows = (
        groups[:, None] == jnp.arange(ctf_table.shape[0], dtype=jnp.int32)[None, :]
    ).astype(jnp.float32)
    ctf_rows = jnp.dot(onehot_rows, ctf_table, precision=lax.Precision.HIGHEST)
    weighted = (
        (chosen.astype(jnp.float32).reshape(count_local, CYCLES, ANG) * ctf_rows[:, :, None])
        .reshape(count_local, CYCLES * ANG)
        .astype(jnp.bfloat16)
    )
    ctf_sq = (ctf_rows * ctf_rows).astype(jnp.bfloat16)
    batch_rows, batch_sq = (
        lax.all_gather(weighted, "cls", axis=0, tiled=True),
        lax.all_gather(ctf_sq, "cls", axis=0, tiled=True),
    )
    batch_major = angle_major(batch_rows)
    doubled = jnp.concatenate([batch_major, batch_major], axis=0)
    refs = classes.astype(jnp.bfloat16)
    refs_major = angle_major(refs)
    cycle_power = jnp.sum(
        jnp.square(refs.astype(jnp.float32)).reshape(classes.shape[0], CYCLES, ANG), axis=2
    )
    block_len = math.gcd(ROT, 6)
    shift_blocks = shifts.reshape(ROT // block_len, block_len)
    scores = all_scores(doubled, refs_major, shift_blocks)
    norm_term = jnp.dot(
        batch_sq.astype(jnp.float32), cycle_power.T, precision=lax.Precision.HIGHEST
    )
    logits = scores - 0.5 * norm_term[None, :, :] + log_prior[None, None, :]
    local_top = jnp.max(logits, axis=(0, 2))
    local_total = jnp.sum(jnp.exp(logits - local_top[None, :, None]), axis=(0, 2))
    row_top, row_total = joined((local_top, local_total), "cls", merge_softmax)
    exp_terms = jnp.exp(logits - row_top[None, :, None])
    weights = (exp_terms / row_total[None, :, None]).astype(jnp.bfloat16)
    log_evidence = row_top + jnp.log(row_total)
    numerator = class_numerator(doubled, weights, shift_blocks)
    weight_sum = jnp.sum(weights.astype(jnp.float32), axis=0)
    denominator = lax.dot_general(
        weight_sum,
        batch_sq.astype(jnp.float32),
        (((0,), (0,)), ((), ())),
        precision=lax.Precision.HIGHEST,
    )
    numerator, denominator = lax.psum((numerator, denominator), "particle")
    spread = jnp.repeat(denominator, ANG, axis=1)
    updated = (1.0 - STEP_WEIGHT) * classes + STEP_WEIGHT * numerator / (spread + PRIOR_WEIGHT)
    return (updated, log_evidence)


def on_device(pool, picks, groups, ctf_table, shifts, classes, log_prior):
    total = classes.shape[0]
    _, full, rest, _ = halves(total)
    quad = lax.axis_size("particle") == 4 and lax.axis_size("cls") == 4
    fits = total % 2 == 0 and QUARTERS * rest <= 8 and 32 <= full <= 48 and total <= ANG
    plan = halved if quad and fits else whole_sum
    return plan(pool, picks, groups, ctf_table, shifts, classes, log_prior)


def solution(mesh):
    in_specs = (
        P(("groups", "particle", "cls"), None),
        P(("groups", "particle", "cls")),
        P(("groups", "particle", "cls")),
        P("groups", None),
        P("groups"),
        P(("groups", "cls"), None),
        P(("groups", "cls")),
    )
    out_specs = (P(("groups", "cls"), None), P(("groups", "particle")))
    return jax.shard_map(
        on_device, mesh=mesh, in_specs=in_specs, out_specs=out_specs, check_vma=False
    )
```

```python
import functools
import math

import jax
import jax.numpy as jnp
from jax import lax
from jax.experimental import pallas as pl
from jax.experimental.pallas import tpu as pltpu
from jax.sharding import PartitionSpec as P

CYCLES = 32
ANG = 128
ROT = 36
PIX = CYCLES * ANG

STEP_WEIGHT = 0.5
PRIOR_WEIGHT = 1.0

VMEM = pl.BlockSpec(memory_space=pltpu.VMEM)
ANY = pl.BlockSpec(memory_space=pl.ANY)
SMEM = pl.BlockSpec(memory_space=pltpu.SMEM)
F32 = jnp.float32
BF16 = jnp.bfloat16
NT = (((1,), (1,)), ((), ()))
TN = (((0,), (0,)), ((), ()))
EXACT = lax.Precision.HIGHEST
NEGATIVE = -1e30
CHUNKS = (8, 8, 8, 8)
LARGE = 58
QUARTERS = 4


def later(kernel, count):
    return lambda *refs: kernel(*refs[count:])


def halves(total):
    half = total // 2
    full = half // 8 * 8
    return half, full, half - full, full + 8


def cost(flops, moved):
    return pl.CostEstimate(flops=int(flops), bytes_accessed=int(moved), transcendentals=0)


def params(mib=8):
    return pltpu.CompilerParams(vmem_limit_bytes=mib * 2**20)


def weigh_kernel(picks, groups, pool, table, out):
    count, stored, ngroup = picks.shape[1], pool.shape[0], table.shape[1]
    pick_hot = (lax.broadcasted_iota(jnp.int32, (stored, count), 0) == picks[...]).astype(F32)
    group_hot = (lax.broadcasted_iota(jnp.int32, (ngroup, count), 0) == groups[...]).astype(F32)
    ctf = jnp.dot(table[...], group_hot, precision=EXACT, preferred_element_type=F32).T
    chosen = lax.dot_general(pick_hot.astype(BF16), pool[...], TN, preferred_element_type=F32)
    for c in range(CYCLES):
        here = slice(c * ANG, (c + 1) * ANG)
        out[:, here] = (chosen[:, here] * ctf[:, c : c + 1]).astype(BF16)
    out[:, PIX:] = jnp.concatenate(
        [ctf * ctf, jnp.zeros((count, ANG - CYCLES), F32)], axis=1
    ).astype(BF16)


def weigh(picks, groups, pool, table):
    count = picks.shape[0]
    return pl.pallas_call(
        weigh_kernel,
        out_shape=jax.ShapeDtypeStruct((count, PIX + ANG), BF16),
        in_specs=[VMEM] * 4,
        out_specs=VMEM,
        compiler_params=params(LARGE),
        cost_estimate=cost(2 * count * 48 * PIX, 2**20),
        name="weigh",
    )(picks.reshape(1, -1), groups.reshape(1, -1), pool, table.T)


def prepare_kernel(width, place, classes, prior, halved, power, column):
    upper = place[0] == 1
    total = classes.shape[0]
    half, full, rest, _ = halves(total)
    none = jnp.zeros((8, ANG), F32)
    pad = jnp.zeros((full + 16 - (total - full), ANG), F32)
    lane = lax.broadcasted_iota(jnp.int32, (width, ANG), 1)

    def mine(low, high):
        high = pltpu.roll(jnp.concatenate([high, pad], axis=0), full + 16 - rest, 0)
        return jnp.where(upper, high[:width], low)

    kept = jnp.zeros((width, ANG), F32)
    for c in range(CYCLES):
        here = slice(c * ANG, (c + 1) * ANG)
        part = mine(classes[0:width, here], classes[full:total, here])
        halved[0 : width + 8, here] = jnp.concatenate([part, none], axis=0).astype(BF16)
        halved[width + 8 :, here] = jnp.concatenate([none, part], axis=0).astype(BF16)
        wide = part.astype(BF16).astype(F32)
        kept = jnp.where(lane == c, jnp.sum(wide * wide, axis=1, keepdims=True), kept)
    power[...] = kept
    turned = jnp.broadcast_to(prior[...], (ANG, ANG)).T
    row = lax.broadcasted_iota(jnp.int32, (width, ANG), 0)
    column[...] = jnp.where(row < half, mine(turned[0:width], turned[full:total]), NEGATIVE)


def prepare(width, place, classes, prior, after):
    return pl.pallas_call(
        later(functools.partial(prepare_kernel, width), len(after)),
        out_shape=(
            jax.ShapeDtypeStruct((2 * (width + 8), PIX), BF16),
            jax.ShapeDtypeStruct((width, ANG), F32),
            jax.ShapeDtypeStruct((width, ANG), F32),
        ),
        in_specs=[ANY] * len(after) + [SMEM, VMEM, VMEM],
        out_specs=(VMEM,) * 3,
        compiler_params=params(LARGE),
        cost_estimate=cost(2 * 2**30, 2 * 2**20),
        name="prepare",
    )(*after, place, classes, prior)


def score_kernel(width, groups, span, place, shifts, halved, power, column, same, across, *refs):
    (terms, summed, stats, sides), (images, logits, *turned) = refs[:4], refs[4:]
    one = same.shape[0]
    count = images.shape[0]
    core = place[2]
    images[pl.ds(pl.multiple_of(core * one, 16), one), :] = same[...]
    images[pl.ds(pl.multiple_of((1 - core) * one, 16), one), :] = across[...]
    squares = images[:, PIX:].astype(F32)
    sides[...] = squares
    norm = lax.dot_general(power[...], squares, NT, precision=EXACT, preferred_element_type=F32)
    bias = column[:, 0:1] - 0.5 * norm

    each = ROT // groups
    top = jnp.full((width, count), NEGATIVE, F32)
    for g in range(groups):
        scores = None
        for q in range(CYCLES // span):
            block = turned[q % 2]
            for c in range(span):
                cycle = q * span + c
                here = slice(cycle * ANG, (cycle + 1) * ANG)
                there = slice(c * ANG, (c + 1) * ANG)
                first, second = halved[: width + 8, here], halved[width + 8 :, here]
                for r in range(0, each, 2):
                    at = r * width
                    one_turned = pltpu.roll(first, shifts[g * each + r], 1)
                    two_turned = pltpu.roll(second, shifts[g * each + r + 1], 1)
                    block[at : at + width - 8, there] = one_turned[: width - 8]
                    block[at + width - 8 : at + width + 8, there] = (
                        one_turned[width - 8 :] + two_turned[:16]
                    )
                    block[at + width + 8 : at + 2 * width, there] = two_turned[16:]
            part = lax.dot_general(
                block[...],
                images[:, q * span * ANG : (q + 1) * span * ANG],
                NT,
                preferred_element_type=F32,
            )
            scores = part if scores is None else scores + part
        for r in range(each):
            value = scores[r * width : (r + 1) * width, :] + bias
            logits[(g * each + r) * width : (g * each + r + 1) * width, :] = value
            top = jnp.maximum(top, value)
    top = jnp.max(top, axis=0, keepdims=True)

    def add(r, sums):
        block = pl.ds(pl.multiple_of(r * 2 * width, 16), 2 * width)
        value = jnp.exp(logits[block, :] - top)
        rounded = value.astype(BF16)
        terms[block, :] = rounded
        kept = rounded.astype(F32)
        return (
            sums[0] + (value[:width] + value[width:]),
            sums[1] + (kept[:width] + kept[width:]),
        )

    zero = jnp.zeros((width, count), F32)
    total, rounded = lax.fori_loop(0, ROT // 2, add, (zero, zero))
    summed[...] = rounded
    stats[0:1, :] = top
    stats[1:2, :] = jnp.sum(total, axis=0, keepdims=True)
    stats[2:, :] = jnp.zeros((6, count), F32)


def score(width, place, shifts, halved, power, column, same, across):
    groups, span = 6,4
    one, full = same.shape
    count = 2 * one
    outs = (
        jax.ShapeDtypeStruct((ROT * width, count), BF16),
        jax.ShapeDtypeStruct((width, count), F32),
        jax.ShapeDtypeStruct((8, count), F32),
        jax.ShapeDtypeStruct((count, ANG), F32),
    )
    return pl.pallas_call(
        functools.partial(score_kernel, width, groups, span),
        out_shape=outs,
        in_specs=[SMEM, SMEM] + [VMEM] * 5,
        out_specs=(VMEM,) * 4,
        scratch_shapes=[pltpu.VMEM((count, full), BF16), pltpu.VMEM((ROT * width, count), F32)]
        + [pltpu.VMEM((ROT // groups * width, span * ANG), BF16)] * 2,
        compiler_params=params(24),
        cost_estimate=cost(10 * 2**30, 20 * 2**20),
        name="score",
    )(place, shifts, halved, power, column, same, across)


def normalize_kernel(place, own, summed, squares, *refs):
    stats, (scales, evidence, denominator, joined) = refs[:-4], refs[-4:]
    count = own.shape[1]
    for m, stat in zip((0, 3, 2, 1), stats):
        joined[pl.ds(pl.multiple_of((place[1] ^ m) * 8, 8), 8), :] = stat[...]
    tops = [joined[8 * j : 8 * j + 1, :] for j in range(len(stats))]
    totals = [joined[8 * j + 1 : 8 * j + 2, :] for j in range(len(stats))]
    top = functools.reduce(jnp.maximum, tops)
    total = sum(t * jnp.exp(h - top) for h, t in zip(tops, totals))
    evidence[...] = jnp.broadcast_to(top + jnp.log(total), (8, count))
    scale = jnp.exp(own[0:1, :] - top) / total
    scales[...] = jnp.broadcast_to(scale, (ANG, count)).T
    denominator[...] = jnp.dot(
        summed[...] * scale, squares[...], precision=EXACT, preferred_element_type=F32
    )


def normalize(place, own, summed, squares, stats):
    width, count = summed.shape
    return pl.pallas_call(
        normalize_kernel,
        out_shape=(
            jax.ShapeDtypeStruct((count, ANG), F32),
            jax.ShapeDtypeStruct((8, count), F32),
            jax.ShapeDtypeStruct((width, ANG), F32),
        ),
        in_specs=[SMEM] + [VMEM] * (3 + len(stats)),
        out_specs=(VMEM,) * 3,
        scratch_shapes=[pltpu.VMEM((8 * len(stats), count), F32)],
        compiler_params=params(),
        cost_estimate=cost(2**30, 2**20),
        name="normalize",
    )(place, own, summed, squares, *stats)


def merge_kernel(place, own, other, out):
    lower = place[2] == 0
    first, second = (jnp.where(lower, a[...], b[...]) for a, b in ((own, other), (other, own)))
    top = jnp.maximum(first[0:1], second[0:1])
    out[...] = jnp.zeros_like(out)
    out[0:1, :] = top
    out[1:2, :] = first[1:2] * jnp.exp(first[0:1] - top) + second[1:2] * jnp.exp(second[0:1] - top)


def merge(place, own, other):
    return pl.pallas_call(
        merge_kernel,
        out_shape=jax.ShapeDtypeStruct(own.shape, F32),
        in_specs=[SMEM, VMEM, VMEM],
        out_specs=VMEM,
        compiler_params=params(4),
        cost_estimate=cost(0, 0),
        name="merge",
    )(place, own, other)


def update_kernel(total, first, span, place, shifts, terms, same, across, scales, *refs):
    below, (out, product) = refs[:-2], refs[-2:]
    _, full, rest, width = halves(total)
    wide = span // QUARTERS
    sent = QUARTERS * full + 8
    lower = place[2] == 0
    part = slice(first * ANG, (first + span) * ANG)
    images = [jnp.where(lower, a[:, part], b[:, part]) for a, b in ((same, across), (across, same))]
    images = jnp.concatenate(images, axis=0).astype(F32)
    scaled = (images * scales[:, 0:1]).astype(BF16)
    product[...] = jnp.dot(terms[...], scaled, preferred_element_type=F32).astype(BF16)
    row = lax.broadcasted_iota(jnp.int32, (8, ANG), 0)
    for i in range(wide):
        there = slice(i * ANG, (i + 1) * ANG)
        tail = jnp.zeros((8, ANG), F32)
        for q in range(QUARTERS):
            j = q * wide + i
            sums = [jnp.zeros((width + 8, ANG), F32)] * 2
            for r in range(ROT):
                back = (ANG - shifts[r]) & (ANG - 1)
                at = r * width - 8 * (r % 2)
                turned = pltpu.roll(product[at : at + width + 8, j * ANG : (j + 1) * ANG], back, 1)
                sums[r % 2] = sums[r % 2] + turned.astype(F32)
            sums = sums[0][:width] + sums[1][8:]
            out[q * full : (q + 1) * full, there] = sums[:full].astype(BF16)
            moved = pltpu.roll(sums[full : full + 8], q * rest, 0) if q else sums[full : full + 8]
            tail = jnp.where((row >= q * rest) & (row < (q + 1) * rest), moved, tail)
        out[sent - 8 : sent, there] = tail.astype(BF16)
    for b in below:
        value = b[0 : full + 8, :]
        high = value.astype(BF16).astype(F32)
        both = high + pltpu.roll(value - high, CYCLES, 1)
        out[sent : sent + 32, 0:ANG] = both[0:32].astype(BF16)
        out[sent : sent + 32, ANG : 2 * ANG] = both[full - 24 : full + 8].astype(BF16)


def update(total, first, cycles, place, shifts, terms, same, across, scales, below, after):
    _, full, _, width = halves(total)
    rows = QUARTERS * full + 8 + 32 * len(below)
    return pl.pallas_call(
        later(functools.partial(update_kernel, total, first, cycles), len(after)),
        out_shape=jax.ShapeDtypeStruct((rows, cycles // QUARTERS * ANG), BF16),
        in_specs=[ANY] * len(after) + [SMEM, SMEM] + [VMEM] * (4 + len(below)),
        out_specs=VMEM,
        scratch_shapes=[pltpu.VMEM((ROT * width, cycles * ANG), BF16)],
        compiler_params=params(20),
        cost_estimate=cost(3 * 2**30, 4 * 2**20),
        name="update",
    )(*after, place, shifts, terms, same, across, scales, *below)


def divide_kernel(total, first, one, two, *refs):
    share, out = refs[0], refs[-1]
    _, full, rest, _ = halves(total)
    sent, wide = out.shape[0], out.shape[1] // ANG
    lane = lax.broadcasted_iota(jnp.int32, (full + 8, ANG), 1)
    row = lax.broadcasted_iota(jnp.int32, (8, ANG), 0)
    if first == 0:
        below = one[sent:, :].astype(F32) + two[sent:, :].astype(F32)
        below = jnp.concatenate([below[0:24, 0:ANG], below[32 - (full - 16) :, ANG:]], axis=0)
        below = below + pltpu.roll(below, ANG - CYCLES, 1)
        share[...] = 1.0 / (below + PRIOR_WEIGHT)
    for i in range(wide):
        there = slice(i * ANG, (i + 1) * ANG)
        tail = jnp.zeros((8, ANG), F32)
        for q in range(QUARTERS):
            cycle = jnp.where(lane == first + q * wide + i, share[...], 0.0)
            factor = jnp.broadcast_to(jnp.sum(cycle, axis=1, keepdims=True), (full + 8, ANG))
            here = slice(q * full, (q + 1) * full)
            sums = one[here, there].astype(F32) + two[here, there].astype(F32)
            out[here, there] = (sums * factor[:full]).astype(BF16)
            moved = pltpu.roll(factor[full:], q * rest, 0) if q else factor[full:]
            tail = jnp.where((row >= q * rest) & (row < (q + 1) * rest), moved, tail)
        sums = one[sent - 8 : sent, there].astype(F32) + two[sent - 8 : sent, there].astype(F32)
        out[sent - 8 : sent, there] = (sums * tail).astype(BF16)


def divide(total, first, cycles, one, two, share, after):
    _, full, _, _ = halves(total)
    outs = () if share else (jax.ShapeDtypeStruct((full + 8, ANG), F32),)
    outs += (jax.ShapeDtypeStruct((QUARTERS * full + 8, cycles // QUARTERS * ANG), BF16),)
    return pl.pallas_call(
        later(functools.partial(divide_kernel, total, first), len(after)),
        out_shape=outs,
        in_specs=[ANY] * len(after) + [VMEM] * (2 + len(share)),
        out_specs=(VMEM,) * len(outs),
        compiler_params=params(8),
        cost_estimate=cost(2**28, 0),
        name="divide",
    )(*after, one, two, *share)


def blend_kernel(chunks, place, classes, *refs):
    out = refs[-1]
    total = classes.shape[0]
    half, full, rest, _ = halves(total)
    upper = place[0] == 1
    done = 0
    for p in range(chunks):
        mine, other = refs[2 * p : 2 * p + 2]
        span = mine.shape[1]
        row = lax.broadcasted_iota(jnp.int32, (full + 16, span), 0)
        none = jnp.zeros((8, span), F32)
        ends = [a[QUARTERS * full :, :].astype(F32) for a in (mine, other)]
        for q in range(QUARTERS):
            rows = []
            for a, end in zip((mine, other), ends):
                end = pltpu.roll(end, 8 - q * rest, 0) if q else end
                rows.append((a[q * full : (q + 1) * full, :].astype(F32), end))
            low, low_end = (jnp.where(upper, b, a) for a, b in zip(*rows))
            high, high_end = (jnp.where(upper, a, b) for a, b in zip(*rows))
            high = pltpu.roll(jnp.concatenate([high, high_end, none], axis=0), rest, 0)
            low_end = jnp.concatenate([low_end, jnp.zeros((full + 8, span), F32)], axis=0)
            upper_rows = jnp.where(row < rest, low_end, high)
            step = jnp.concatenate([low, upper_rows[: total - full]], axis=0)
            at = slice(done, done + span)
            done += span
            out[:, at] = (1.0 - STEP_WEIGHT) * classes[:, at] + STEP_WEIGHT * step


def blend(first, place, classes, updates, before):
    span = QUARTERS * sum(mine.shape[1] for mine, _ in updates)
    block = pl.BlockSpec((classes.shape[0], span), lambda i: (0, first * ANG // span))
    flat = [u for pair in updates for u in pair]
    return pl.pallas_call(
        functools.partial(blend_kernel, len(updates)),
        grid=(1,),
        out_shape=jax.ShapeDtypeStruct(classes.shape, F32),
        in_specs=[SMEM, block]
        + [pl.BlockSpec(u.shape, lambda i: (0, 0)) for u in flat]
        + [ANY] * len(before),
        out_specs=block,
        input_output_aliases={2 + len(flat): 0} if before else {},
        compiler_params=params(),
        cost_estimate=cost(2**30, 2**20),
        name="blend",
    )(place, classes, *flat, *before)


def halved(pool, picks, groups, ctf_table, shifts, classes, log_prior):
    total = classes.shape[0]
    width = halves(total)[-1]
    axes = ("particle", "cls")
    z, cls = lax.axis_index("particle"), lax.axis_index("cls")
    chip, core = cls // 2, cls % 2
    half = z % 2
    place = jnp.stack([half, half * 2 + chip, core]).astype(jnp.int32)
    prior = jnp.pad(log_prior, (0, ANG - total)).reshape(1, ANG)

    def swap(a, mask):
        return lax.ppermute(a, axes, [(i, i ^ mask) for i in range(16)])

    CORE, CHIP, NEXT, SAME = 1, 2, 4, 8

    own = weigh(picks, groups, pool, ctf_table)
    beside = swap(own, NEXT)
    own_x = swap(own, CHIP)
    beside_x = swap(own, NEXT + CHIP)
    halved, power, column = prepare(width, place, classes, prior, (own,))
    own_x, beside, beside_x, halved = lax.optimization_barrier((own_x, beside, beside_x, halved))
    pairs = [
        (jnp.where(chip == 1, x, a), jnp.where(chip == 1, a, x))
        for a, x in ((own, own_x), (beside, beside_x))
    ]
    odd = z % 2 == 1
    low = [jnp.where(odd, b, a) for a, b in zip(*pairs)]
    high = [jnp.where(odd, a, b) for a, b in zip(*pairs)]
    same = jnp.concatenate(low + high, axis=0)
    across = swap(same, CORE)

    terms, summed, own_stat, squares = score(
        width, place, shifts, halved, power, column, same, across
    )

    stat = merge(place, own_stat, swap(own_stat, CORE))
    stats = [stat] + [swap(stat, m) for m in (CHIP, NEXT, NEXT + CHIP)]
    stats = [stats[j] for j in (0, 3, 2, 1)]
    scales, evidence, below = normalize(place, own_stat, summed, squares, stats)

    mine, other, ratios, others, share = [], [], [], [], []
    last = len(CHUNKS) - 1
    firsts = [sum(CHUNKS[:p]) for p in range(len(CHUNKS))]

    def finish(p):
        after = tuple(ratios[-1:])
        *new, ratio = divide(total, firsts[p], CHUNKS[p], mine[p], other[p], tuple(share), after)
        share.extend(new)
        ratios.append(ratio)
        others.append(swap(ratios[p], NEXT))

    for p, cycles in enumerate(CHUNKS):
        after, extra = tuple(mine[-1:]), () if p else (below,)
        part = update(
            total, firsts[p], cycles, place, shifts, terms, same, across, scales, extra, after
        )
        mine.append(part)
        other.append(swap(part, SAME))
    for p in range(last + 1):
        finish(p)
    both = list(zip(ratios, others))
    cut = 2
    updated = blend(0, place, classes, both[:cut], ())
    updated = blend(firsts[cut], place, classes, both[cut:], (updated,))
    count = picks.shape[0]
    by_shard = evidence[0].reshape(2, 2, 2, count)
    log_evidence = jnp.take(by_shard, z % 2, axis=1)
    return (updated, jnp.transpose(log_evidence, (1, 0, 2)).reshape(4 * count))


def joined(part, axis, combine):
    gathered = jax.tree.map(lambda a: lax.all_gather(a, axis), part)

    def take(source):
        return jax.tree.map(lambda a: lax.dynamic_index_in_dim(a, source, 0, False), gathered)

    return lax.fori_loop(
        1, lax.axis_size(axis), lambda source, state: combine(state, take(source)), take(0)
    )


def angle_major(images):
    count_rows = images.shape[0]
    return jnp.transpose(images.reshape(count_rows, CYCLES, ANG), (2, 1, 0)).reshape(
        ANG * CYCLES, count_rows
    )


def turned_view(doubled, offset):
    return lax.dynamic_slice_in_dim(doubled, offset * CYCLES, ANG * CYCLES, 0)


def all_scores(doubled, refs_major, shift_blocks):
    block_len = shift_blocks.shape[1]

    def single(shift_row):
        outputs = []
        for slot in range(block_len):
            piece = turned_view(doubled, shift_row[slot])
            outputs.append(
                lax.dot_general(
                    piece, refs_major, (((0,), (0,)), ((), ())), preferred_element_type=jnp.float32
                )
            )
        return jnp.stack(outputs, axis=0)

    partial_value = lax.map(single, shift_blocks)
    return partial_value.reshape(-1, partial_value.shape[2], partial_value.shape[3])


def class_numerator(doubled, weights, shift_blocks):
    nblocks, block_len = shift_blocks.shape
    weight_blocks = weights.reshape(nblocks, block_len, weights.shape[1], weights.shape[2])

    def advance(carried, pieces):
        shift_row, weight_block = pieces
        for slot in range(block_len):
            piece = turned_view(doubled, shift_row[slot])
            carried = carried + jnp.dot(
                piece, weight_block[slot], preferred_element_type=jnp.float32
            )
        return (carried, None)

    start_value = jnp.zeros((ANG * CYCLES, weights.shape[2]), jnp.float32)
    numerator_major, _ = lax.scan(advance, start_value, (shift_blocks, weight_blocks))
    classes_here = weights.shape[2]
    return jnp.transpose(numerator_major.reshape(ANG, CYCLES, classes_here), (2, 1, 0)).reshape(
        classes_here, CYCLES * ANG
    )


def merge_softmax(earlier, later):
    row_top = jnp.maximum(earlier[0], later[0])
    row_total = earlier[1] * jnp.exp(earlier[0] - row_top) + later[1] * jnp.exp(later[0] - row_top)
    return (row_top, row_total)


def whole_sum(pool, picks, groups, ctf_table, shifts, classes, log_prior):
    chosen = jnp.take(pool, picks, axis=0)
    count_local = chosen.shape[0]
    onehot_rows = (
        groups[:, None] == jnp.arange(ctf_table.shape[0], dtype=jnp.int32)[None, :]
    ).astype(jnp.float32)
    ctf_rows = jnp.dot(onehot_rows, ctf_table, precision=lax.Precision.HIGHEST)
    weighted = (
        (chosen.astype(jnp.float32).reshape(count_local, CYCLES, ANG) * ctf_rows[:, :, None])
        .reshape(count_local, CYCLES * ANG)
        .astype(jnp.bfloat16)
    )
    ctf_sq = (ctf_rows * ctf_rows).astype(jnp.bfloat16)
    batch_rows, batch_sq = (
        lax.all_gather(weighted, "cls", axis=0, tiled=True),
        lax.all_gather(ctf_sq, "cls", axis=0, tiled=True),
    )
    batch_major = angle_major(batch_rows)
    doubled = jnp.concatenate([batch_major, batch_major], axis=0)
    refs = classes.astype(jnp.bfloat16)
    refs_major = angle_major(refs)
    cycle_power = jnp.sum(
        jnp.square(refs.astype(jnp.float32)).reshape(classes.shape[0], CYCLES, ANG), axis=2
    )
    block_len = math.gcd(ROT, 6)
    shift_blocks = shifts.reshape(ROT // block_len, block_len)
    scores = all_scores(doubled, refs_major, shift_blocks)
    norm_term = jnp.dot(
        batch_sq.astype(jnp.float32), cycle_power.T, precision=lax.Precision.HIGHEST
    )
    logits = scores - 0.5 * norm_term[None, :, :] + log_prior[None, None, :]
    local_top = jnp.max(logits, axis=(0, 2))
    local_total = jnp.sum(jnp.exp(logits - local_top[None, :, None]), axis=(0, 2))
    row_top, row_total = joined((local_top, local_total), "cls", merge_softmax)
    exp_terms = jnp.exp(logits - row_top[None, :, None])
    weights = (exp_terms / row_total[None, :, None]).astype(jnp.bfloat16)
    log_evidence = row_top + jnp.log(row_total)
    numerator = class_numerator(doubled, weights, shift_blocks)
    weight_sum = jnp.sum(weights.astype(jnp.float32), axis=0)
    denominator = lax.dot_general(
        weight_sum,
        batch_sq.astype(jnp.float32),
        (((0,), (0,)), ((), ())),
        precision=lax.Precision.HIGHEST,
    )
    numerator, denominator = lax.psum((numerator, denominator), "particle")
    spread = jnp.repeat(denominator, ANG, axis=1)
    updated = (1.0 - STEP_WEIGHT) * classes + STEP_WEIGHT * numerator / (spread + PRIOR_WEIGHT)
    return (updated, log_evidence)


def on_device(pool, picks, groups, ctf_table, shifts, classes, log_prior):
    total = classes.shape[0]
    _, full, rest, _ = halves(total)
    quad = lax.axis_size("particle") == 4 and lax.axis_size("cls") == 4
    fits = total % 2 == 0 and QUARTERS * rest <= 8 and full % 16 == 0 and 32 <= full <= 48 and total <= ANG
    plan = halved if quad and fits else whole_sum
    return plan(pool, picks, groups, ctf_table, shifts, classes, log_prior)


def solution(mesh):
    in_specs = (
        P(("groups", "particle", "cls"), None),
        P(("groups", "particle", "cls")),
        P(("groups", "particle", "cls")),
        P("groups", None),
        P("groups"),
        P(("groups", "cls"), None),
        P(("groups", "cls")),
    )
    out_specs = (P(("groups", "cls"), None), P(("groups", "particle")))
    return jax.shard_map(
        on_device, mesh=mesh, in_specs=in_specs, out_specs=out_specs, check_vma=False
    )
```
